128 devices in a mesh: dom: 4 (over y_lo, core), cell: 32 (over x, y_hi, z).
Axes of the slice: x: 4, y: 4 (y_hi: 2, y_lo: 2; y = y_hi * 2 + y_lo), z: 4, core: 2. Of those that a mesh axis runs over, the one named last changes fastest.
Arguments:
- particles: float32 [512, 262144], P('dom', 'cell'), may hold values from -20 to 20
- gradients: float32 [512, 262144], P('dom', 'cell'), may hold values from -0.0034179688 to 0.0034179688
- width: float32 [1], replicated, may hold values from 655360 to 917504
- step_size: float32 [1], replicated, may hold values from 262144 to 524288
Outputs:
- moved: float32 [512, 262144], P('dom', 'cell')
The draws below stay inside these ranges and needn't reach their ends.
All inputs are finite; a program needn't handle non-finite values.
Results may differ from the reference program's by a relative error of at most 0.000068.
Values sent between devices are 32-bit elements; how exact they have to be, the bound alone decides.
A program may use at most 128 MiB of HBM per device.

```python
import jax
import jax.numpy as jnp
from jax import lax

PARTICLES = 512
CELLS = 262144


def draw_particles(key, part):
    key = jax.random.fold_in(key, 11)
    key_noise = jax.random.fold_in(key, 0)
    key_scale = jax.random.fold_in(key, 1)
    key_mix = jax.random.fold_in(key, 3)
    key_sign = jax.random.fold_in(key, 4)
    cell_pos = jnp.arange(CELLS, dtype=jnp.float32) / CELLS
    cell_ramp = jnp.sqrt(0.5 + cell_pos)[None, :]
    scales = jnp.exp(jax.random.uniform(key_scale, (PARTICLES, 1), jnp.float32, jnp.log(0.6), jnp.log(1.6)))
    noise_base = jax.random.truncated_normal(key_noise, -4.0, 4.0, (PARTICLES, CELLS), jnp.float32)
    magnitudes = jnp.exp(jax.random.uniform(key_mix, (16,), jnp.float32, jnp.log(0.5), 0.0))
    sign_values = (2 * jax.random.randint(key_sign, (16,), 0, 2) - 1).astype(jnp.float32)
    mix_weights = sign_values * magnitudes * jnp.sqrt(1.49 / jnp.sum(magnitudes * magnitudes))
    mixture = mix_weights[0] * noise_base
    for member in range(1, 16):
        shuffle_rows = jax.random.permutation(jax.random.fold_in(key_mix, member + 100), PARTICLES)
        mixture = mixture + mix_weights[member] * noise_base[shuffle_rows]
    coupled = 7.0 * jnp.tanh(mixture / 7.0)
    return (scales * cell_ramp * coupled).astype(jnp.float32)


def shard_levels(stream_key, extent, cuts, smallest, top_value):
    gain = 1.0
    for dim, blocks in cuts:
        draws = jax.random.uniform(jax.random.fold_in(jax.random.fold_in(stream_key, 6), dim), (blocks,), jnp.float32, smallest / len(cuts), top_value / len(cuts))
        gain = gain * jnp.repeat(jnp.exp(draws), extent[dim] // blocks).reshape((-1,) + (1,) * (len(extent) - 1 - dim))
    return gain


def gaussian(stream_key, dims, scale, bound, pieces=(), kind=jnp.bfloat16):
    gain = shard_levels(stream_key, dims, pieces, -0.22, 0.18) if pieces else 1.0
    drawn = jax.random.normal(stream_key, dims, jnp.float32) * scale * gain
    return jnp.minimum(jnp.maximum(drawn, -bound), bound).astype(kind)


def setup_inputs(seed: int = 0) -> dict:
    seeds = jax.random.split(jax.random.key(seed), 5)
    return {
        "particles": draw_particles(jax.random.fold_in(seeds[4], 71), 0),
        "gradients": gaussian(seeds[1], (PARTICLES, CELLS), (60.0 / CELLS), 0.0034179688, ((0, 4), (1, 32)), jnp.float32),
        "width": jnp.clip(jax.random.uniform(seeds[2], (1,), jnp.float32, 655360.0, 917504.0), 655360.0, 917504.0),
        "step_size": jnp.clip(jax.random.uniform(seeds[3], (1,), jnp.float32, 262144.0, 524288.0), 262144.0, 524288.0),
    }


def reference(particles, gradients, width, step_size):
    inv_band = 1.0 / width[0]
    sq_norms = jnp.sum(particles * particles, axis=1)
    inner_prod = lax.dot_general(particles, particles, (((1,), (1,)), ((), ())), precision=lax.Precision.HIGHEST, preferred_element_type=jnp.float32)
    distance = sq_norms[:, None] + sq_norms[None, :] - 2.0 * inner_prod
    kernel = jnp.exp(-distance * inv_band)
    rowsum = jnp.sum(kernel, axis=1)
    shifted = gradients - 2.0 * inv_band * particles
    attracted = jnp.dot(kernel, shifted, precision=lax.Precision.HIGHEST, preferred_element_type=jnp.float32)
    velocity = (attracted + 2.0 * inv_band * particles * rowsum[:, None]) / PARTICLES
    return particles + step_size[0] * velocity
```

```python
import functools

import jax
import jax.numpy as jnp
from jax import lax
from jax.experimental import pallas as pl
from jax.experimental.pallas import tpu as pltpu
from jax.sharding import PartitionSpec as P

MESH = pl.DeviceIdType.MESH
HIGHEST = lax.Precision.HIGHEST
NX, NYH, NZ = 4, 2, 4
GRAM_PARTS = 4
STEP_PARTS = 16
EARLY_PARTS = 6


def kernel(
    dims,
    width_ref,
    step_ref,
    particles,
    gradients,
    moved,
    x_own,
    s_own,
    x_gram,
    x_chip,
    s_all,
    result,
    part,
    sum_core,
    sum_x,
    sum_z,
    sum_y,
    inner,
    weights,
    load_sem,
    x_send,
    x_recv,
    xc_sem,
    ss_sem,
    s_send,
    s_recv,
    red_sem,
    own_sem,
    out_send,
    out_recv,
):
    rows, cells, nx, nz = dims
    every = 4 * rows
    half, quarter = cells // 2, cells // 4
    gram_cols, step_cols = quarter // GRAM_PARTS, half // STEP_PARTS
    dom, cell = lax.axis_index("dom"), lax.axis_index("cell")
    hi, lo = dom // 2, lax.rem(dom, 2)
    cx, cy, cz = cell // (NYH * nz), lax.rem(cell // nz, NYH), lax.rem(cell, nz)

    def cell_of(x, y, z):
        return (x * NYH + y) * nz + z

    sibling = (hi * 2 + 1 - lo, cell)
    across = [((1 - hi) * 2, cell), ((1 - hi) * 2 + 1, cell)]
    along_x = [lax.rem(cx + d, nx) for d in range(1, nx)]
    along_z = [lax.rem(cz + d, nz) for d in range(1, nz)]
    x_peers = [(dom, cell_of(x, cy, cz)) for x in along_x]
    z_peers = [(dom, cell_of(cx, cy, z)) for z in along_z]
    y_near = ((1 - hi) * 2 + lo, cell_of(cx, 1 - cy, cz))
    y_pair = ((1 - hi) * 2 + lo, cell)

    def send(src, dst, sems, to):
        return pltpu.make_async_remote_copy(
            src_ref=src,
            dst_ref=dst,
            send_sem=sems[0],
            recv_sem=sems[1],
            device_id=to,
            device_id_type=MESH,
        )

    def rows_of(index, count):
        return pl.ds(pl.multiple_of(index, count), count)

    def cols_of(index, count):
        return pl.ds(pl.multiple_of(index, count), count)

    my_rows = rows_of(dom * rows, rows)
    loads = [
        pltpu.make_async_copy(particles, x_own, load_sem.at[0]),
        pltpu.make_async_copy(gradients, s_own, load_sem.at[1]),
        pltpu.make_async_copy(
            particles.at[:, cols_of(half * lo + quarter * hi, quarter)],
            x_gram.at[my_rows],
            load_sem.at[2],
        ),
        pltpu.make_async_copy(
            particles.at[:, cols_of(half * lo, half)],
            x_chip.at[rows_of(lo * rows, rows)],
            load_sem.at[3],
        ),
    ]
    for load in loads:
        load.start()

    barrier = pltpu.get_barrier_semaphore()
    greeted = [sibling, *across, *x_peers, *z_peers, y_near]
    for peer in greeted:
        pl.semaphore_signal(barrier, inc=1, device_id=peer, device_id_type=MESH)
    pl.semaphore_wait(barrier, len(greeted))

    def gram_copy(slot, c):
        to = (across + [sibling])[slot]
        to_hi, to_lo = (hi, 1 - lo) if slot == 2 else (1 - hi, slot)
        start = half * to_lo + quarter * to_hi + gram_cols * c
        sem = lo if slot < 2 else 2
        return pltpu.make_async_remote_copy(
            src_ref=particles.at[:, cols_of(start, gram_cols)],
            dst_ref=x_gram.at[my_rows, cols_of(gram_cols * c, gram_cols)],
            send_sem=x_send.at[slot, c],
            recv_sem=x_recv.at[sem, c],
            device_id=to,
            device_id_type=MESH,
        )

    def gram_recv(sem, c):
        block = x_gram.at[pl.ds(0, rows), cols_of(gram_cols * c, gram_cols)]
        return pltpu.make_async_copy(block, block, x_recv.at[sem, c])

    for c in range(GRAM_PARTS):
        for slot in range(3):
            gram_copy(slot, c).start()
    x_swap = send(
        particles.at[:, cols_of(half * (1 - lo), half)],
        x_chip.at[rows_of(lo * rows, rows)],
        (xc_sem.at[0], xc_sem.at[1]),
        sibling,
    )
    x_swap.start()

    inv_band = 1.0 / width_ref[0]
    loads[0].wait()
    loads[1].wait()

    @pl.loop(0, STEP_PARTS * 2)
    def _(u):
        cols = cols_of(u * step_cols, step_cols)
        s_own[:, cols] = s_own[:, cols] - 2.0 * inv_band * x_own[:, cols]

    def step_copy(slot, u):
        return pltpu.make_async_remote_copy(
            src_ref=s_own.at[:, cols_of(half * slot + step_cols * u, step_cols)],
            dst_ref=s_all.at[my_rows, cols_of(step_cols * u, step_cols)],
            send_sem=s_send.at[slot, u],
            recv_sem=s_recv.at[lo, u],
            device_id=across[slot],
            device_id_type=MESH,
        )

    def step_recv(sem, u):
        block = s_all.at[pl.ds(0, rows), cols_of(step_cols * u, step_cols)]
        return pltpu.make_async_copy(block, block, s_recv.at[sem, u])

    @pl.loop(0, EARLY_PARTS)
    def _(u):
        for slot in range(2):
            step_copy(slot, u).start()

    s_swap = send(
        s_own.at[:, cols_of(half * (1 - lo), half)],
        s_all.at[my_rows],
        (ss_sem.at[0], ss_sem.at[1]),
        sibling,
    )
    s_swap.start()
    s_keep = pltpu.make_async_copy(
        s_own.at[:, cols_of(half * lo, half)], s_all.at[my_rows], load_sem.at[4]
    )
    s_keep.start()

    loads[2].wait()
    part[...] = jnp.zeros_like(part)

    @pl.loop(0, GRAM_PARTS)
    def _(c):
        for sem in range(3):
            if sem == 2:
                gram_recv(2, c).wait()
            else:
                gram_recv(sem, c).wait()
        block = x_gram[:, cols_of(gram_cols * c, gram_cols)]
        part[...] += lax.dot_general(
            block,
            block,
            (((1,), (1,)), ((), ())),
            precision=HIGHEST,
            preferred_element_type=jnp.float32,
        )

    n_core, n_x, n_z = every // 2, every // 2 // nx, every // 2 // nx // nz
    count = [0]

    def sems():
        k = count[0]
        count[0] += 1
        return red_sem.at[0, k], red_sem.at[1, k]

    swap = send(part.at[rows_of((1 - lo) * n_core, n_core)], sum_core, sems(), sibling)
    swap.start()
    swap.wait()
    sum_core[...] += part[rows_of(lo * n_core, n_core), :]

    copies = [
        send(sum_core.at[rows_of(x * n_x, n_x)], sum_x.at[d], sems(), peer)
        for d, (x, peer) in enumerate(zip(along_x, x_peers, strict=True))
    ]
    for copy in copies:
        copy.start()
    total = sum_core[rows_of(cx * n_x, n_x), :]
    for d, copy in enumerate(copies):
        copy.wait()
        total = total + sum_x[d]
    sum_x[nx - 1] = total

    copies = [
        send(sum_x.at[nx - 1, rows_of(z * n_z, n_z)], sum_z.at[d], sems(), peer)
        for d, (z, peer) in enumerate(zip(along_z, z_peers, strict=True))
    ]
    for copy in copies:
        copy.start()
    total = sum_x[nx - 1, rows_of(cz * n_z, n_z), :]
    for d, copy in enumerate(copies):
        copy.wait()
        total = total + sum_z[d]
    sum_y[0] = total
    swap = send(sum_y.at[0], sum_y.at[1], sems(), y_near)
    swap.start()
    swap.wait()
    sum_y[2] = sum_y[0] + sum_y[1]
    swap = send(sum_y.at[2], sum_y.at[3], sems(), y_pair)
    swap.start()

    @pl.loop(EARLY_PARTS, STEP_PARTS)
    def _(u):
        for slot in range(2):
            step_copy(slot, u).start()

    swap.wait()
    z_rows = rows_of(lo * n_core + cx * n_x + cz * n_z, n_z)
    inner[z_rows, :] = sum_y[2] + sum_y[3]
    copies = [send(inner.at[z_rows], inner.at[z_rows], sems(), peer) for peer in z_peers]
    for copy in copies:
        copy.start()
    for copy in copies:
        copy.wait()
    x_rows = rows_of(lo * n_core + cx * n_x, n_x)
    copies = [send(inner.at[x_rows], inner.at[x_rows], sems(), peer) for peer in x_peers]
    for copy in copies:
        copy.start()
    for copy in copies:
        copy.wait()
    core_rows = rows_of(lo * n_core, n_core)
    swap = send(inner.at[core_rows], inner.at[core_rows], sems(), sibling)
    swap.start()
    swap.wait()

    products = inner[...]
    i = lax.broadcasted_iota(jnp.int32, (every, every), 0)
    j = lax.broadcasted_iota(jnp.int32, (every, every), 1)
    all_norms = jnp.sum(jnp.where(i == j, products, 0.0), axis=0, keepdims=True)
    near = inner[rows_of(hi * 2 * rows, 2 * rows), :]
    i = lax.broadcasted_iota(jnp.int32, (2 * rows, every), 0) + hi * 2 * rows
    j = lax.broadcasted_iota(jnp.int32, (2 * rows, every), 1)
    own_norms = jnp.sum(jnp.where(i == j, near, 0.0), axis=1, keepdims=True)
    distance = own_norms + all_norms - 2.0 * near
    weights[...] = jnp.exp(-distance * inv_band)

    step_size = step_ref[0]
    pull = 2.0 * inv_band * jnp.sum(weights[...], axis=1, keepdims=True)
    loads[3].wait()
    x_swap.wait()
    s_swap.wait()
    s_keep.wait()

    def out_own(u):
        cols = cols_of(step_cols * u, step_cols)
        return pltpu.make_async_copy(
            result.at[rows_of(lo * rows, rows), cols],
            moved.at[:, cols_of(half * lo + step_cols * u, step_cols)],
            own_sem.at[u],
        )

    def out_swap(u):
        cols = cols_of(step_cols * u, step_cols)
        return send(
            result.at[rows_of((1 - lo) * rows, rows), cols],
            moved.at[:, cols_of(half * lo + step_cols * u, step_cols)],
            (out_send.at[u], out_recv.at[u]),
            sibling,
        )

    @pl.loop(0, STEP_PARTS)
    def _(u):
        for sem in range(2):
            step_recv(sem, u).wait()
        cols = cols_of(step_cols * u, step_cols)
        attracted = jnp.dot(
            weights[...],
            s_all[:, cols],
            precision=HIGHEST,
            preferred_element_type=jnp.float32,
        )
        x = x_chip[:, cols]
        result[:, cols] = x + step_size * ((attracted + pull * x) * (1.0 / every))
        out_own(u).start()
        out_swap(u).start()

    @pl.loop(0, STEP_PARTS)
    def _(u):
        for slot in range(2):
            step_copy(slot, u).wait_send()
        out_own(u).wait()
        out_swap(u).wait()

    @pl.loop(0, GRAM_PARTS)
    def _(c):
        for slot in range(3):
            gram_copy(slot, c).wait_send()


def on_device(dims, width, step_size, particles, gradients):
    rows, cells, nx, nz = dims
    every, half = 4 * rows, cells // 2
    n_core = every // 2
    n_x = n_core // nx
    n_z = n_x // nz
    f32 = jnp.float32
    sem = pltpu.SemaphoreType.DMA
    messages = 4 + 2 * (nx - 1) + 2 * (nz - 1)
    return pl.pallas_call(
        functools.partial(kernel, dims),
        out_shape=jax.ShapeDtypeStruct((rows, cells), f32),
        in_specs=[pl.BlockSpec(memory_space=pltpu.SMEM)] * 2 + [pl.BlockSpec(memory_space=pl.ANY)] * 2,
        out_specs=pl.BlockSpec(memory_space=pl.ANY),
        scratch_shapes=[
            pltpu.VMEM((rows, cells), f32),
            pltpu.VMEM((rows, cells), f32),
            pltpu.VMEM((every, cells // 4), f32),
            pltpu.VMEM((2 * rows, half), f32),
            pltpu.VMEM((every, half), f32),
            pltpu.VMEM((2 * rows, half), f32),
            pltpu.VMEM((every, every), f32),
            pltpu.VMEM((n_core, every), f32),
            pltpu.VMEM((nx, n_x, every), f32),
            pltpu.VMEM((nz, n_z, every), f32),
            pltpu.VMEM((4, n_z, every), f32),
            pltpu.VMEM((every, every), f32),
            pltpu.VMEM((2 * rows, every), f32),
            sem((5,)),
            sem((3, GRAM_PARTS)),
            sem((3, GRAM_PARTS)),
            sem((2,)),
            sem((2,)),
            sem((2, STEP_PARTS)),
            sem((2, STEP_PARTS)),
            sem((2, messages)),
            sem((STEP_PARTS,)),
            sem((STEP_PARTS,)),
            sem((STEP_PARTS,)),
        ],
        compiler_params=pltpu.CompilerParams(
            collective_id=0, has_side_effects=True, vmem_limit_bytes=60 * 2**20
        ),
        cost_estimate=pl.CostEstimate(
            flops=4 * every * every * cells // 4,
            bytes_accessed=5 * 4 * rows * cells,
            transcendentals=2 * rows * every,
        ),
    )(width, step_size, particles, gradients)


def solution(mesh):
    def step(particles, gradients, width, step_size):
        rows, cells = particles.shape
        nz = NZ if mesh.shape["cell"] == NX * NYH * NZ else 1
        nx = mesh.shape["cell"] // NYH // nz
        return on_device((rows, cells, nx, nz), width, step_size, particles, gradients)

    in_specs = (P("dom", "cell"), P("dom", "cell"), P(), P())
    out_specs = P("dom", "cell")
    return jax.shard_map(step, mesh=mesh, in_specs=in_specs, out_specs=out_specs, check_vma=False)
```

```python
import functools

import jax
import jax.numpy as jnp
from jax import lax
from jax.experimental import pallas as pl
from jax.experimental.pallas import tpu as pltpu
from jax.sharding import PartitionSpec as P

MESH = pl.DeviceIdType.MESH
HIGHEST = lax.Precision.HIGHEST
NX, NYH, NZ = 4, 2, 4
GRAM_PARTS = 4
STEP_PARTS = 16
MAIN_PARTS = STEP_PARTS - 1
EARLY_PARTS = 6


def kernel(
    dims,
    width_hbm,
    step_hbm,
    particles,
    gradients,
    moved,
    x_own,
    s_own,
    x_gram,
    x_chip,
    s_all,
    result,
    product,
    far,
    part,
    sum_core,
    sum_x,
    sum_z,
    sum_y,
    inner,
    width_ref,
    step_ref,
    ready,
    load_sem,
    x_send,
    x_recv,
    xc_sem,
    ss_sem,
    s_send,
    s_recv,
    red_sem,
    out_send,
    out_recv,
    far_send,
    far_recv,
):
    rows, cells, nx, nz = dims
    every = 4 * rows
    half, quarter = cells // 2, cells // 4
    gram_cols, step_cols = quarter // GRAM_PARTS, half // STEP_PARTS
    dom, cell = lax.axis_index("dom"), lax.axis_index("cell")
    hi, lo = dom // 2, lax.rem(dom, 2)
    cx, cy, cz = cell // (NYH * nz), lax.rem(cell // nz, NYH), lax.rem(cell, nz)

    def cell_of(x, y, z):
        return (x * NYH + y) * nz + z

    sibling = (hi * 2 + 1 - lo, cell)
    across = [((1 - hi) * 2, cell), ((1 - hi) * 2 + 1, cell)]
    along_x = [lax.rem(cx + d, nx) for d in range(1, nx)]
    along_z = [lax.rem(cz + d, nz) for d in range(1, nz)]
    x_peers = [(dom, cell_of(x, cy, cz)) for x in along_x]
    z_peers = [(dom, cell_of(cx, cy, z)) for z in along_z]
    y_near = ((1 - hi) * 2 + lo, cell_of(cx, 1 - cy, cz))
    y_pair = ((1 - hi) * 2 + lo, cell)

    def send(src, dst, sems, to):
        return pltpu.make_async_remote_copy(
            src_ref=src,
            dst_ref=dst,
            send_sem=sems[0],
            recv_sem=sems[1],
            device_id=to,
            device_id_type=MESH,
        )

    def rows_of(index, count):
        return pl.ds(pl.multiple_of(index, count), count)

    def cols_of(index, count):
        return pl.ds(pl.multiple_of(index, count), count)

    def signal(sem, to):
        pl.semaphore_signal(sem, inc=1, device_id=to, device_id_type=MESH)

    barrier = pltpu.get_barrier_semaphore()
    signal(barrier, across[0])

    @pl.when(lo == 1)
    def _():
        signal(barrier, sibling)

    my_rows = rows_of(dom * rows, rows)
    loads = [
        pltpu.make_async_copy(particles, x_own, load_sem.at[0]),
        pltpu.make_async_copy(gradients, s_own, load_sem.at[1]),
        pltpu.make_async_copy(
            particles.at[:, cols_of(half * lo + quarter * hi, quarter)],
            x_gram.at[my_rows],
            load_sem.at[2],
        ),
        pltpu.make_async_copy(
            particles.at[:, cols_of(half * lo, half)],
            x_chip.at[rows_of(lo * rows, rows)],
            load_sem.at[3],
        ),
        pltpu.make_async_copy(width_hbm, width_ref, load_sem.at[5]),
        pltpu.make_async_copy(step_hbm, step_ref, load_sem.at[6]),
    ]
    for load in loads:
        load.start()

    @pl.when(lo == 0)
    def _():
        pl.semaphore_wait(barrier, 3)
        signal(ready, sibling)
        signal(ready, across[1])

    @pl.when(lo == 1)
    def _():
        for peer in [*x_peers, *z_peers, y_near]:
            signal(barrier, peer)
        pl.semaphore_wait(ready, 2)

    def gram_copy(slot, c):
        to = (across + [sibling])[slot]
        to_hi, to_lo = (hi, 1 - lo) if slot == 2 else (1 - hi, slot)
        start = half * to_lo + quarter * to_hi + gram_cols * c
        sem = lo if slot < 2 else 2
        return pltpu.make_async_remote_copy(
            src_ref=particles.at[:, cols_of(start, gram_cols)],
            dst_ref=x_gram.at[my_rows, cols_of(gram_cols * c, gram_cols)],
            send_sem=x_send.at[slot, c],
            recv_sem=x_recv.at[sem, c],
            device_id=to,
            device_id_type=MESH,
        )

    def gram_recv(sem, c):
        block = x_gram.at[pl.ds(0, rows), cols_of(gram_cols * c, gram_cols)]
        return pltpu.make_async_copy(block, block, x_recv.at[sem, c])

    for c in range(GRAM_PARTS):
        for slot in range(3):
            gram_copy(slot, c).start()
    x_swap = send(
        particles.at[:, cols_of(half * (1 - lo), half)],
        x_chip.at[rows_of(lo * rows, rows)],
        (xc_sem.at[0], xc_sem.at[1]),
        sibling,
    )
    x_swap.start()

    loads[4].wait()
    loads[5].wait()
    inv_band = 1.0 / width_ref[0, 0]
    loads[0].wait()
    loads[1].wait()

    @pl.loop(0, STEP_PARTS * 2)
    def _(u):
        cols = cols_of(u * step_cols, step_cols)
        s_own[:, cols] = s_own[:, cols] - 2.0 * inv_band * x_own[:, cols]

    def step_copy(slot, u):
        return pltpu.make_async_remote_copy(
            src_ref=s_own.at[:, cols_of(half * slot + step_cols * u, step_cols)],
            dst_ref=s_all.at[my_rows, cols_of(step_cols * u, step_cols)],
            send_sem=s_send.at[slot, u],
            recv_sem=s_recv.at[lo, u],
            device_id=across[slot],
            device_id_type=MESH,
        )

    def step_recv(sem, u):
        block = s_all.at[pl.ds(0, rows), cols_of(step_cols * u, step_cols)]
        return pltpu.make_async_copy(block, block, s_recv.at[sem, u])

    @pl.loop(0, EARLY_PARTS)
    def _(u):
        for slot in range(2):
            step_copy(slot, u).start()

    s_swap = send(
        s_own.at[:, cols_of(half * (1 - lo), half)],
        s_all.at[my_rows],
        (ss_sem.at[0], ss_sem.at[1]),
        sibling,
    )
    s_swap.start()
    s_keep = pltpu.make_async_copy(
        s_own.at[:, cols_of(half * lo, half)], s_all.at[my_rows], load_sem.at[4]
    )
    s_keep.start()

    loads[2].wait()
    part[...] = jnp.zeros_like(part)

    @pl.loop(0, GRAM_PARTS)
    def _(c):
        for sem in range(3):
            if sem == 2:
                gram_recv(2, c).wait()
            else:
                gram_recv(sem, c).wait()
        block = x_gram[:, cols_of(gram_cols * c, gram_cols)]
        part[...] += lax.dot_general(
            block,
            block,
            (((1,), (1,)), ((), ())),
            precision=HIGHEST,
            preferred_element_type=jnp.float32,
        )

    n_x, n_z, n_y = every // nx, every // nx // nz, every // nx // nz // 2
    count = [0]

    def sems():
        k = count[0]
        count[0] += 1
        return red_sem.at[0, k], red_sem.at[1, k]

    def later_parts():
        @pl.loop(EARLY_PARTS, MAIN_PARTS)
        def _(u):
            for slot in range(2):
                step_copy(slot, u).start()

    to_core = send(part, sum_core, sems(), sibling)
    from_core = send(inner, inner, sems(), sibling)

    @pl.when(lo == 0)
    def _():
        to_core.start()
        to_core.wait_send()
        later_parts()
        from_core.wait_recv()

    @pl.when(lo == 1)
    def _():
        pl.semaphore_wait(barrier, len(x_peers) + len(z_peers) + 1)
        to_core.wait_recv()
        sum_core[...] += part[...]
        copies = [
            send(sum_core.at[rows_of(x * n_x, n_x)], sum_x.at[d], sems(), peer)
            for d, (x, peer) in enumerate(zip(along_x, x_peers, strict=True))
        ]
        for copy in copies:
            copy.start()
        total = sum_core[rows_of(cx * n_x, n_x), :]
        for d, copy in enumerate(copies):
            copy.wait()
            total = total + sum_x[d]
        sum_x[nx - 1] = total

        copies = [
            send(sum_x.at[nx - 1, rows_of(z * n_z, n_z)], sum_z.at[d], sems(), peer)
            for d, (z, peer) in enumerate(zip(along_z, z_peers, strict=True))
        ]
        for copy in copies:
            copy.start()
        total = sum_x[nx - 1, rows_of(cz * n_z, n_z), :]
        for d, copy in enumerate(copies):
            copy.wait()
            total = total + sum_z[d]
        sum_z[nz - 1] = total

        swap = send(sum_z.at[nz - 1, rows_of((1 - cy) * n_y, n_y)], sum_y.at[0], sems(), y_near)
        swap.start()
        swap.wait()
        sum_y[1] = sum_y[0] + sum_z[nz - 1, rows_of(cy * n_y, n_y), :]
        swap = send(sum_y.at[1], sum_y.at[2], sems(), y_pair)
        swap.start()
        later_parts()
        swap.wait()
        y_rows = rows_of(cx * n_x + cz * n_z + cy * n_y, n_y)
        z_rows = rows_of(cx * n_x + cz * n_z, n_z)
        x_rows = rows_of(cx * n_x, n_x)
        inner[y_rows, :] = sum_y[1] + sum_y[2]
        for block, peers in ((y_rows, [y_near]), (z_rows, z_peers), (x_rows, x_peers)):
            copies = [send(inner.at[block], inner.at[block], sems(), peer) for peer in peers]
            for copy in copies:
                copy.start()
            for copy in copies:
                copy.wait()
        from_core.start()
        from_core.wait_send()

    products = inner[...]
    i = lax.broadcasted_iota(jnp.int32, (every, every), 0)
    j = lax.broadcasted_iota(jnp.int32, (every, every), 1)
    norms = jnp.where(i == j, products, 0.0)
    distance = (
        jnp.sum(norms, axis=1, keepdims=True)
        + jnp.sum(norms, axis=0, keepdims=True)
        - 2.0 * products
    )
    inner[...] = jnp.exp(-distance * inv_band)
    near_rows = rows_of(hi * 2 * rows, 2 * rows)
    far_rows = rows_of((1 - hi) * 2 * rows, 2 * rows)
    near_cols = cols_of(hi * 2 * rows, 2 * rows)

    def dot(left, right):
        return jnp.dot(left, right, precision=HIGHEST, preferred_element_type=jnp.float32)

    s_swap.wait()
    s_keep.wait()
    last = step_cols * MAIN_PARTS
    last_cols = pl.ds(last, step_cols)
    product[...] = dot(inner[far_rows, near_cols], s_all[near_rows, last_cols])
    far_copies = [
        send(product.at[pl.ds(slot * rows, rows)], far.at[lo], (far_send.at[slot], far_recv.at[lo]), across[slot])
        for slot in range(2)
    ]
    for copy in far_copies:
        copy.start()

    step_size = step_ref[0, 0]
    pull = 2.0 * inv_band * jnp.sum(inner[near_rows, :], axis=1, keepdims=True)
    loads[3].wait()
    x_swap.wait()

    def out_cols(u):
        return cols_of(half * lo + step_cols * u, step_cols)

    def out_swap(u):
        return send(
            result.at[rows_of((1 - lo) * rows, rows), cols_of(step_cols * u, step_cols)],
            moved.at[:, out_cols(u)],
            (out_send.at[u], out_recv.at[u]),
            sibling,
        )

    def finish(u, attracted):
        cols = cols_of(step_cols * u, step_cols)
        x = x_chip[:, cols]
        result[:, cols] = x + step_size * ((attracted + pull * x) * (1.0 / every))
        out_swap(u).start()
        moved[:, out_cols(u)] = result[rows_of(lo * rows, rows), cols]

    finish(MAIN_PARTS, dot(inner[near_rows, near_cols], s_all[near_rows, last_cols]))

    @pl.loop(0, MAIN_PARTS)
    def _(u):
        for sem in range(2):
            step_recv(sem, u).wait()
        finish(u, dot(inner[near_rows, :], s_all[:, cols_of(step_cols * u, step_cols)]))

    @pl.loop(0, MAIN_PARTS)
    def _(u):
        for slot in range(2):
            step_copy(slot, u).wait_send()

    @pl.loop(0, GRAM_PARTS)
    def _(c):
        for slot in range(3):
            gram_copy(slot, c).wait_send()

    @pl.loop(0, STEP_PARTS)
    def _(u):
        out_swap(u).wait()

    for slot in range(2):
        pltpu.make_async_copy(far.at[slot], far.at[slot], far_recv.at[slot]).wait()
        cols = pl.ds(half * slot + last, step_cols)
        moved[:, cols] = moved[:, cols] + step_size * (far[slot] * (1.0 / every))
    for copy in far_copies:
        copy.wait_send()


def on_device(dims, width, step_size, particles, gradients):
    rows, cells, nx, nz = dims
    every, half = 4 * rows, cells // 2
    n_x = every // nx
    n_z = n_x // nz
    f32 = jnp.float32
    sem = pltpu.SemaphoreType.DMA
    messages = 5 + 2 * (nx - 1) + 2 * (nz - 1)
    return pl.pallas_call(
        functools.partial(kernel, dims),
        out_shape=pltpu.VMEM((rows, cells), f32),
        in_specs=[pl.BlockSpec(memory_space=pltpu.HBM)] * 4,
        out_specs=pl.BlockSpec(memory_space=pltpu.VMEM),
        scratch_shapes=[
            pltpu.VMEM((rows, cells), f32),
            pltpu.VMEM((rows, cells), f32),
            pltpu.VMEM((every, cells // 4), f32),
            pltpu.VMEM((2 * rows, half), f32),
            pltpu.VMEM((every, half), f32),
            pltpu.VMEM((2 * rows, half), f32),
            pltpu.VMEM((2 * rows, half // STEP_PARTS), f32),
            pltpu.VMEM((2, rows, half // STEP_PARTS), f32),
            pltpu.VMEM((every, every), f32),
            pltpu.VMEM((every, every), f32),
            pltpu.VMEM((nx, n_x, every), f32),
            pltpu.VMEM((nz, n_z, every), f32),
            pltpu.VMEM((3, n_z // 2, every), f32),
            pltpu.VMEM((every, every), f32),
            pltpu.SMEM((1, 1), f32),
            pltpu.SMEM((1, 1), f32),
            pltpu.SemaphoreType.REGULAR,
            sem((7,)),
            sem((3, GRAM_PARTS)),
            sem((3, GRAM_PARTS)),
            sem((2,)),
            sem((2,)),
            sem((2, STEP_PARTS)),
            sem((2, STEP_PARTS)),
            sem((2, messages)),
            sem((STEP_PARTS,)),
            sem((STEP_PARTS,)),
            sem((2,)),
            sem((2,)),
        ],
        compiler_params=pltpu.CompilerParams(
            collective_id=0, has_side_effects=True, vmem_limit_bytes=52 * 2**20
        ),
        cost_estimate=pl.CostEstimate(
            flops=4 * every * every * cells // 4,
            bytes_accessed=5 * 4 * rows * cells,
            transcendentals=2 * rows * every,
        ),
    )(
        width.reshape(1, 1),
        step_size.reshape(1, 1),
        particles,
        gradients,
    )


def solution(mesh):
    def step(particles, gradients, width, step_size):
        rows, cells = particles.shape
        nz = NZ if mesh.shape["cell"] == NX * NYH * NZ else 1
        nx = mesh.shape["cell"] // NYH // nz
        return on_device((rows, cells, nx, nz), width, step_size, particles, gradients)

    in_specs = (P("dom", "cell"), P("dom", "cell"), P(), P())
    out_specs = P("dom", "cell")
    return jax.shard_map(step, mesh=mesh, in_specs=in_specs, out_specs=out_specs, check_vma=False)
```

```python
import functools

import jax
import jax.numpy as jnp
from jax import lax
from jax.experimental import pallas as pl
from jax.experimental.pallas import tpu as pltpu
from jax.sharding import PartitionSpec as P

MESH = pl.DeviceIdType.MESH
HIGHEST = lax.Precision.HIGHEST
NX, NYH, NZ = 4, 2, 4
GRAM_PARTS = 4
STEP_PARTS = 16
MAIN_PARTS = STEP_PARTS - 1
EARLY_PARTS = 6


def kernel(
    dims,
    width_hbm,
    step_hbm,
    particles,
    gradients,
    moved,
    x_own,
    s_own,
    x_gram,
    x_chip,
    s_all,
    result,
    product,
    far,
    part,
    sum_core,
    sum_x,
    sum_z,
    sum_y,
    inner,
    width_ref,
    step_ref,
    ready,
    load_sem,
    x_send,
    x_recv,
    xc_sem,
    ss_sem,
    s_send,
    s_recv,
    red_sem,
    out_send,
    out_recv,
    far_send,
    far_recv,
):
    rows, cells, nx, nz = dims
    every = 4 * rows
    half, quarter = cells // 2, cells // 4
    gram_cols, step_cols = quarter // GRAM_PARTS, half // STEP_PARTS
    dom, cell = lax.axis_index("dom"), lax.axis_index("cell")
    hi, lo = dom // 2, lax.rem(dom, 2)
    cx, cy, cz = cell // (NYH * nz), lax.rem(cell // nz, NYH), lax.rem(cell, nz)

    def cell_of(x, y, z):
        return (x * NYH + y) * nz + z

    sibling = (hi * 2 + 1 - lo, cell)
    across = [((1 - hi) * 2, cell), ((1 - hi) * 2 + 1, cell)]
    along_x = [lax.rem(cx + d, nx) for d in range(1, nx)]
    along_z = [lax.rem(cz + d, nz) for d in range(1, nz)]
    x_peers = [(dom, cell_of(x, cy, cz)) for x in along_x]
    z_peers = [(dom, cell_of(cx, cy, z)) for z in along_z]
    y_near = ((1 - hi) * 2 + lo, cell_of(cx, 1 - cy, cz))
    y_pair = ((1 - hi) * 2 + lo, cell)

    def send(src, dst, sems, to):
        return pltpu.make_async_remote_copy(
            src_ref=src,
            dst_ref=dst,
            send_sem=sems[0],
            recv_sem=sems[1],
            device_id=to,
            device_id_type=MESH,
        )

    def rows_of(index, count):
        return pl.ds(pl.multiple_of(index, count), count)

    def cols_of(index, count):
        return pl.ds(pl.multiple_of(index, count), count)

    def signal(sem, to):
        pl.semaphore_signal(sem, inc=1, device_id=to, device_id_type=MESH)

    cross_peers = [*x_peers, *z_peers, y_near]
    barrier = pltpu.get_barrier_semaphore()
    signal(barrier, y_pair)

    @pl.when(lo == 0)
    def _():
        for peer in cross_peers:
            signal(barrier, peer)

    my_rows = rows_of(dom * rows, rows)
    loads = [
        pltpu.make_async_copy(particles, x_own, load_sem.at[0]),
        pltpu.make_async_copy(gradients, s_own, load_sem.at[1]),
        pltpu.make_async_copy(
            particles.at[:, cols_of(half * lo + quarter * hi, quarter)],
            x_gram.at[my_rows],
            load_sem.at[2],
        ),
        pltpu.make_async_copy(
            particles.at[:, cols_of(half * lo, half)],
            x_chip.at[rows_of(lo * rows, rows)],
            load_sem.at[3],
        ),
        pltpu.make_async_copy(width_hbm, width_ref, load_sem.at[5]),
        pltpu.make_async_copy(step_hbm, step_ref, load_sem.at[6]),
    ]
    for load in loads:
        load.start()

    def gram_copy(slot, c):
        to = (across + [sibling])[slot]
        to_hi, to_lo = (hi, 1 - lo) if slot == 2 else (1 - hi, slot)
        start = half * to_lo + quarter * to_hi + gram_cols * c
        sem = lo if slot < 2 else 2
        return pltpu.make_async_remote_copy(
            src_ref=particles.at[:, cols_of(start, gram_cols)],
            dst_ref=x_gram.at[my_rows, cols_of(gram_cols * c, gram_cols)],
            send_sem=x_send.at[slot, c],
            recv_sem=x_recv.at[sem, c],
            device_id=to,
            device_id_type=MESH,
        )

    def gram_recv(sem, c):
        block = x_gram.at[pl.ds(0, rows), cols_of(gram_cols * c, gram_cols)]
        return pltpu.make_async_copy(block, block, x_recv.at[sem, c])

    @pl.when(lo == 1)
    def _():
        pl.semaphore_wait(barrier, 1)
        for c in range(GRAM_PARTS):
            gram_copy(1, c).start()
        signal(barrier, sibling)
        pl.semaphore_wait(ready, 1)

    @pl.when(lo == 0)
    def _():
        pl.semaphore_wait(barrier, 2 + len(cross_peers))
        signal(ready, sibling)
        for c in range(GRAM_PARTS):
            gram_copy(1, c).start()

    for c in range(GRAM_PARTS):
        gram_copy(0, c).start()
        gram_copy(2, c).start()
    x_swap = send(
        particles.at[:, cols_of(half * (1 - lo), half)],
        x_chip.at[rows_of(lo * rows, rows)],
        (xc_sem.at[0], xc_sem.at[1]),
        sibling,
    )
    x_swap.start()

    loads[4].wait()
    loads[5].wait()
    inv_band = 1.0 / width_ref[0, 0]
    loads[0].wait()
    loads[1].wait()

    @pl.loop(0, STEP_PARTS * 2)
    def _(u):
        cols = cols_of(u * step_cols, step_cols)
        s_own[:, cols] = s_own[:, cols] - 2.0 * inv_band * x_own[:, cols]

    def step_copy(slot, u):
        return pltpu.make_async_remote_copy(
            src_ref=s_own.at[:, cols_of(half * slot + step_cols * u, step_cols)],
            dst_ref=s_all.at[my_rows, cols_of(step_cols * u, step_cols)],
            send_sem=s_send.at[slot, u],
            recv_sem=s_recv.at[lo, u],
            device_id=across[slot],
            device_id_type=MESH,
        )

    def step_recv(sem, u):
        block = s_all.at[pl.ds(0, rows), cols_of(step_cols * u, step_cols)]
        return pltpu.make_async_copy(block, block, s_recv.at[sem, u])

    @pl.loop(0, EARLY_PARTS)
    def _(u):
        for slot in range(2):
            step_copy(slot, u).start()

    s_swap = send(
        s_own.at[:, cols_of(half * (1 - lo), half)],
        s_all.at[my_rows],
        (ss_sem.at[0], ss_sem.at[1]),
        sibling,
    )
    s_swap.start()
    s_keep = pltpu.make_async_copy(
        s_own.at[:, cols_of(half * lo, half)], s_all.at[my_rows], load_sem.at[4]
    )
    s_keep.start()

    loads[2].wait()
    part[...] = jnp.zeros_like(part)

    @pl.loop(0, GRAM_PARTS)
    def _(c):
        for sem in range(3):
            if sem == 2:
                gram_recv(2, c).wait()
            else:
                gram_recv(sem, c).wait()
        block = x_gram[:, cols_of(gram_cols * c, gram_cols)]
        part[...] += lax.dot_general(
            block,
            block,
            (((1,), (1,)), ((), ())),
            precision=HIGHEST,
            preferred_element_type=jnp.float32,
        )

    n_x, n_z, n_y = every // nx, every // nx // nz, every // nx // nz // 2
    count = [0]

    def sems():
        k = count[0]
        count[0] += 1
        return red_sem.at[0, k], red_sem.at[1, k]

    def later_parts():
        @pl.loop(EARLY_PARTS, MAIN_PARTS)
        def _(u):
            for slot in range(2):
                step_copy(slot, u).start()

    to_core = send(part, sum_core, sems(), sibling)
    from_core = send(inner, inner, sems(), sibling)

    @pl.when(lo == 1)
    def _():
        to_core.start()
        to_core.wait_send()
        later_parts()
        from_core.wait_recv()

    @pl.when(lo == 0)
    def _():
        to_core.wait_recv()
        sum_core[...] += part[...]
        copies = [
            send(sum_core.at[rows_of(x * n_x, n_x)], sum_x.at[d], sems(), peer)
            for d, (x, peer) in enumerate(zip(along_x, x_peers, strict=True))
        ]
        for copy in copies:
            copy.start()
        total = sum_core[rows_of(cx * n_x, n_x), :]
        for d, copy in enumerate(copies):
            copy.wait()
            total = total + sum_x[d]
        sum_x[nx - 1] = total

        copies = [
            send(sum_x.at[nx - 1, rows_of(z * n_z, n_z)], sum_z.at[d], sems(), peer)
            for d, (z, peer) in enumerate(zip(along_z, z_peers, strict=True))
        ]
        for copy in copies:
            copy.start()
        total = sum_x[nx - 1, rows_of(cz * n_z, n_z), :]
        for d, copy in enumerate(copies):
            copy.wait()
            total = total + sum_z[d]
        sum_z[nz - 1] = total

        swap = send(sum_z.at[nz - 1, rows_of((1 - cy) * n_y, n_y)], sum_y.at[0], sems(), y_near)
        swap.start()
        swap.wait()
        sum_y[1] = sum_y[0] + sum_z[nz - 1, rows_of(cy * n_y, n_y), :]
        swap = send(sum_y.at[1], sum_y.at[2], sems(), y_pair)
        swap.start()
        later_parts()
        swap.wait()
        y_rows = rows_of(cx * n_x + cz * n_z + cy * n_y, n_y)
        z_rows = rows_of(cx * n_x + cz * n_z, n_z)
        x_rows = rows_of(cx * n_x, n_x)
        inner[y_rows, :] = sum_y[1] + sum_y[2]
        for block, peers in ((y_rows, [y_near]), (z_rows, z_peers), (x_rows, x_peers)):
            copies = [send(inner.at[block], inner.at[block], sems(), peer) for peer in peers]
            for copy in copies:
                copy.start()
            for copy in copies:
                copy.wait()
        from_core.start()
        from_core.wait_send()

    products = inner[...]
    i = lax.broadcasted_iota(jnp.int32, (every, every), 0)
    j = lax.broadcasted_iota(jnp.int32, (every, every), 1)
    norms = jnp.where(i == j, products, 0.0)
    distance = (
        jnp.sum(norms, axis=1, keepdims=True)
        + jnp.sum(norms, axis=0, keepdims=True)
        - 2.0 * products
    )
    inner[...] = jnp.exp(-distance * inv_band)
    near_rows = rows_of(hi * 2 * rows, 2 * rows)
    far_rows = rows_of((1 - hi) * 2 * rows, 2 * rows)
    near_cols = cols_of(hi * 2 * rows, 2 * rows)

    def dot(left, right):
        return jnp.dot(left, right, precision=HIGHEST, preferred_element_type=jnp.float32)

    s_swap.wait()
    s_keep.wait()
    last = step_cols * MAIN_PARTS
    last_cols = pl.ds(last, step_cols)
    product[...] = dot(inner[far_rows, near_cols], s_all[near_rows, last_cols])
    far_copies = [
        send(product.at[pl.ds(slot * rows, rows)], far.at[lo], (far_send.at[slot], far_recv.at[lo]), across[slot])
        for slot in range(2)
    ]
    for copy in far_copies:
        copy.start()

    step_size = step_ref[0, 0]
    pull = 2.0 * inv_band * jnp.sum(inner[near_rows, :], axis=1, keepdims=True)
    loads[3].wait()
    x_swap.wait()

    def out_cols(u):
        return cols_of(half * lo + step_cols * u, step_cols)

    def out_swap(u):
        return send(
            result.at[rows_of((1 - lo) * rows, rows), cols_of(step_cols * u, step_cols)],
            moved.at[:, out_cols(u)],
            (out_send.at[u], out_recv.at[u]),
            sibling,
        )

    def finish(u, attracted):
        cols = cols_of(step_cols * u, step_cols)
        x = x_chip[:, cols]
        result[:, cols] = x + step_size * ((attracted + pull * x) * (1.0 / every))
        out_swap(u).start()
        moved[:, out_cols(u)] = result[rows_of(lo * rows, rows), cols]

    finish(MAIN_PARTS, dot(inner[near_rows, near_cols], s_all[near_rows, last_cols]))

    @pl.loop(0, MAIN_PARTS)
    def _(u):
        for sem in range(2):
            step_recv(sem, u).wait()
        finish(u, dot(inner[near_rows, :], s_all[:, cols_of(step_cols * u, step_cols)]))

    @pl.loop(0, MAIN_PARTS)
    def _(u):
        for slot in range(2):
            step_copy(slot, u).wait_send()

    @pl.loop(0, GRAM_PARTS)
    def _(c):
        for slot in range(3):
            gram_copy(slot, c).wait_send()

    @pl.loop(0, STEP_PARTS)
    def _(u):
        out_swap(u).wait()

    for slot in range(2):
        pltpu.make_async_copy(far.at[slot], far.at[slot], far_recv.at[slot]).wait()
        cols = pl.ds(half * slot + last, step_cols)
        moved[:, cols] = moved[:, cols] + step_size * (far[slot] * (1.0 / every))
    for copy in far_copies:
        copy.wait_send()


def on_device(dims, width, step_size, particles, gradients):
    rows, cells, nx, nz = dims
    every, half = 4 * rows, cells // 2
    n_x = every // nx
    n_z = n_x // nz
    f32 = jnp.float32
    sem = pltpu.SemaphoreType.DMA
    messages = 5 + 2 * (nx - 1) + 2 * (nz - 1)
    return pl.pallas_call(
        functools.partial(kernel, dims),
        out_shape=pltpu.VMEM((rows, cells), f32),
        in_specs=[pl.BlockSpec(memory_space=pltpu.HBM)] * 4,
        out_specs=pl.BlockSpec(memory_space=pltpu.VMEM),
        scratch_shapes=[
            pltpu.VMEM((rows, cells), f32),
            pltpu.VMEM((rows, cells), f32),
            pltpu.VMEM((every, cells // 4), f32),
            pltpu.VMEM((2 * rows, half), f32),
            pltpu.VMEM((every, half), f32),
            pltpu.VMEM((2 * rows, half), f32),
            pltpu.VMEM((2 * rows, half // STEP_PARTS), f32),
            pltpu.VMEM((2, rows, half // STEP_PARTS), f32),
            pltpu.VMEM((every, every), f32),
            pltpu.VMEM((every, every), f32),
            pltpu.VMEM((nx, n_x, every), f32),
            pltpu.VMEM((nz, n_z, every), f32),
            pltpu.VMEM((3, n_z // 2, every), f32),
            pltpu.VMEM((every, every), f32),
            pltpu.SMEM((1, 1), f32),
            pltpu.SMEM((1, 1), f32),
            pltpu.SemaphoreType.REGULAR,
            sem((7,)),
            sem((3, GRAM_PARTS)),
            sem((3, GRAM_PARTS)),
            sem((2,)),
            sem((2,)),
            sem((2, STEP_PARTS)),
            sem((2, STEP_PARTS)),
            sem((2, messages)),
            sem((STEP_PARTS,)),
            sem((STEP_PARTS,)),
            sem((2,)),
            sem((2,)),
        ],
        compiler_params=pltpu.CompilerParams(
            collective_id=0, has_side_effects=True, vmem_limit_bytes=52 * 2**20
        ),
        cost_estimate=pl.CostEstimate(
            flops=4 * every * every * cells // 4,
            bytes_accessed=5 * 4 * rows * cells,
            transcendentals=2 * rows * every,
        ),
    )(
        width.reshape(1, 1),
        step_size.reshape(1, 1),
        particles,
        gradients,
    )


def solution(mesh):
    def step(particles, gradients, width, step_size):
        rows, cells = particles.shape
        nz = NZ if mesh.shape["cell"] == NX * NYH * NZ else 1
        nx = mesh.shape["cell"] // NYH // nz
        return on_device((rows, cells, nx, nz), width, step_size, particles, gradients)

    in_specs = (P("dom", "cell"), P("dom", "cell"), P(), P())
    out_specs = P("dom", "cell")
    return jax.shard_map(step, mesh=mesh, in_specs=in_specs, out_specs=out_specs, check_vma=False)
```

```python
import functools

import jax
import jax.numpy as jnp
from jax import lax
from jax.experimental import pallas as pl
from jax.experimental.pallas import tpu as pltpu
from jax.sharding import PartitionSpec as P

MESH = pl.DeviceIdType.MESH
HIGHEST = lax.Precision.HIGHEST
NX, NYH, NZ = 4, 2, 4
GRAM_PARTS = 4
STEP_PARTS = 16
MAIN_PARTS = STEP_PARTS - 1
EARLY_PARTS = 6


def kernel(
    dims,
    width_hbm,
    step_hbm,
    particles,
    gradients,
    moved,
    x_own,
    s_own,
    x_gram,
    x_chip,
    s_all,
    result,
    product,
    far,
    part,
    sum_core,
    sum_x,
    sum_z,
    sum_y,
    inner,
    width_ref,
    step_ref,
    ready,
    load_sem,
    x_send,
    x_recv,
    xc_sem,
    ss_sem,
    s_send,
    s_recv,
    red_sem,
    out_send,
    out_recv,
    far_send,
    far_recv,
):
    rows, cells, nx, nz = dims
    every = 4 * rows
    half, quarter = cells // 2, cells // 4
    gram_cols, step_cols = quarter // GRAM_PARTS, half // STEP_PARTS
    dom, cell = lax.axis_index("dom"), lax.axis_index("cell")
    hi, lo = dom // 2, lax.rem(dom, 2)
    cx, cy, cz = cell // (NYH * nz), lax.rem(cell // nz, NYH), lax.rem(cell, nz)

    def cell_of(x, y, z):
        return (x * NYH + y) * nz + z

    sibling = (hi * 2 + 1 - lo, cell)
    across = [((1 - hi) * 2, cell), ((1 - hi) * 2 + 1, cell)]
    along_x = [lax.rem(cx + d, nx) for d in range(1, nx)]
    along_z = [lax.rem(cz + d, nz) for d in range(1, nz)]
    x_peers = [(dom, cell_of(x, cy, cz)) for x in along_x]
    z_peers = [(dom, cell_of(cx, cy, z)) for z in along_z]
    y_near = ((1 - hi) * 2 + lo, cell_of(cx, 1 - cy, cz))
    y_pair = ((1 - hi) * 2 + lo, cell)

    def send(src, dst, sems, to):
        return pltpu.make_async_remote_copy(
            src_ref=src,
            dst_ref=dst,
            send_sem=sems[0],
            recv_sem=sems[1],
            device_id=to,
            device_id_type=MESH,
        )

    def rows_of(index, count):
        return pl.ds(pl.multiple_of(index, count), count)

    def cols_of(index, count):
        return pl.ds(pl.multiple_of(index, count), count)

    def signal(sem, to):
        pl.semaphore_signal(sem, inc=1, device_id=to, device_id_type=MESH)

    cross_peers = [*x_peers, *z_peers, y_near]
    barrier = pltpu.get_barrier_semaphore()
    signal(barrier, y_pair)

    @pl.when(lo == 0)
    def _():
        for peer in cross_peers:
            signal(barrier, peer)

    my_rows = rows_of(dom * rows, rows)
    loads = [
        pltpu.make_async_copy(particles, x_own, load_sem.at[0]),
        pltpu.make_async_copy(gradients, s_own, load_sem.at[1]),
        pltpu.make_async_copy(
            particles.at[:, cols_of(half * lo + quarter * hi, quarter)],
            x_gram.at[my_rows],
            load_sem.at[2],
        ),
        pltpu.make_async_copy(
            particles.at[:, cols_of(half * lo, half)],
            x_chip.at[rows_of(lo * rows, rows)],
            load_sem.at[3],
        ),
        pltpu.make_async_copy(width_hbm, width_ref, load_sem.at[5]),
        pltpu.make_async_copy(step_hbm, step_ref, load_sem.at[6]),
    ]
    def gram_copy(slot, c):
        to = (across + [sibling])[slot]
        to_hi, to_lo = (hi, 1 - lo) if slot == 2 else (1 - hi, slot)
        start = half * to_lo + quarter * to_hi + gram_cols * c
        sem = lo if slot < 2 else 2
        return pltpu.make_async_remote_copy(
            src_ref=particles.at[:, cols_of(start, gram_cols)],
            dst_ref=x_gram.at[my_rows, cols_of(gram_cols * c, gram_cols)],
            send_sem=x_send.at[slot, c],
            recv_sem=x_recv.at[sem, c],
            device_id=to,
            device_id_type=MESH,
        )

    def gram_recv(sem, c):
        block = x_gram.at[pl.ds(0, rows), cols_of(gram_cols * c, gram_cols)]
        return pltpu.make_async_copy(block, block, x_recv.at[sem, c])

    @pl.when(lo == 1)
    def _():
        pl.semaphore_wait(barrier, 1)
        signal(barrier, sibling)
        for c in range(GRAM_PARTS):
            gram_copy(1, c).start()
        pl.semaphore_wait(ready, 1)

    @pl.when(lo == 0)
    def _():
        pl.semaphore_wait(barrier, 2 + len(cross_peers))
        signal(ready, sibling)
        for c in range(GRAM_PARTS):
            gram_copy(1, c).start()

    for c in range(GRAM_PARTS):
        gram_copy(0, c).start()
        gram_copy(2, c).start()
    for load in loads:
        load.start()
    x_swap = send(
        particles.at[:, cols_of(half * (1 - lo), half)],
        x_chip.at[rows_of(lo * rows, rows)],
        (xc_sem.at[0], xc_sem.at[1]),
        sibling,
    )
    x_swap.start()

    loads[4].wait()
    loads[5].wait()
    inv_band = 1.0 / width_ref[0, 0]
    loads[0].wait()
    loads[1].wait()

    @pl.loop(0, STEP_PARTS * 2)
    def _(u):
        cols = cols_of(u * step_cols, step_cols)
        s_own[:, cols] = s_own[:, cols] - 2.0 * inv_band * x_own[:, cols]

    def step_copy(slot, u):
        return pltpu.make_async_remote_copy(
            src_ref=s_own.at[:, cols_of(half * slot + step_cols * u, step_cols)],
            dst_ref=s_all.at[my_rows, cols_of(step_cols * u, step_cols)],
            send_sem=s_send.at[slot, u],
            recv_sem=s_recv.at[lo, u],
            device_id=across[slot],
            device_id_type=MESH,
        )

    def step_recv(sem, u):
        block = s_all.at[pl.ds(0, rows), cols_of(step_cols * u, step_cols)]
        return pltpu.make_async_copy(block, block, s_recv.at[sem, u])

    @pl.loop(0, EARLY_PARTS)
    def _(u):
        for slot in range(2):
            step_copy(slot, u).start()

    s_swap = send(
        s_own.at[:, cols_of(half * (1 - lo), half)],
        s_all.at[my_rows],
        (ss_sem.at[0], ss_sem.at[1]),
        sibling,
    )
    s_swap.start()
    s_keep = pltpu.make_async_copy(
        s_own.at[:, cols_of(half * lo, half)], s_all.at[my_rows], load_sem.at[4]
    )
    s_keep.start()

    loads[2].wait()
    part[...] = jnp.zeros_like(part)

    @pl.loop(0, GRAM_PARTS)
    def _(c):
        for sem in range(3):
            if sem == 2:
                gram_recv(2, c).wait()
            else:
                gram_recv(sem, c).wait()
        block = x_gram[:, cols_of(gram_cols * c, gram_cols)]
        part[...] += lax.dot_general(
            block,
            block,
            (((1,), (1,)), ((), ())),
            precision=HIGHEST,
            preferred_element_type=jnp.float32,
        )

    n_x, n_z, n_y = every // nx, every // nx // nz, every // nx // nz // 2
    count = [0]

    def sems():
        k = count[0]
        count[0] += 1
        return red_sem.at[0, k], red_sem.at[1, k]

    def later_parts():
        @pl.loop(EARLY_PARTS, MAIN_PARTS)
        def _(u):
            for slot in range(2):
                step_copy(slot, u).start()

    to_core = send(part, sum_core, sems(), sibling)
    from_core = send(inner, inner, sems(), sibling)

    @pl.when(lo == 1)
    def _():
        to_core.start()
        to_core.wait_send()
        later_parts()
        from_core.wait_recv()

    @pl.when(lo == 0)
    def _():
        to_core.wait_recv()
        sum_core[...] += part[...]
        copies = [
            send(sum_core.at[rows_of(x * n_x, n_x)], sum_x.at[d], sems(), peer)
            for d, (x, peer) in enumerate(zip(along_x, x_peers, strict=True))
        ]
        for copy in copies:
            copy.start()
        total = sum_core[rows_of(cx * n_x, n_x), :]
        for d, copy in enumerate(copies):
            copy.wait()
            total = total + sum_x[d]
        sum_x[nx - 1] = total

        copies = [
            send(sum_x.at[nx - 1, rows_of(z * n_z, n_z)], sum_z.at[d], sems(), peer)
            for d, (z, peer) in enumerate(zip(along_z, z_peers, strict=True))
        ]
        for copy in copies:
            copy.start()
        total = sum_x[nx - 1, rows_of(cz * n_z, n_z), :]
        for d, copy in enumerate(copies):
            copy.wait()
            total = total + sum_z[d]
        sum_z[nz - 1] = total

        swap = send(sum_z.at[nz - 1, rows_of((1 - cy) * n_y, n_y)], sum_y.at[0], sems(), y_near)
        swap.start()
        swap.wait()
        sum_y[1] = sum_y[0] + sum_z[nz - 1, rows_of(cy * n_y, n_y), :]
        swap = send(sum_y.at[1], sum_y.at[2], sems(), y_pair)
        swap.start()
        later_parts()
        swap.wait()
        y_rows = rows_of(cx * n_x + cz * n_z + cy * n_y, n_y)
        z_rows = rows_of(cx * n_x + cz * n_z, n_z)
        x_rows = rows_of(cx * n_x, n_x)
        inner[y_rows, :] = sum_y[1] + sum_y[2]
        for block, peers in ((y_rows, [y_near]), (z_rows, z_peers), (x_rows, x_peers)):
            copies = [send(inner.at[block], inner.at[block], sems(), peer) for peer in peers]
            for copy in copies:
                copy.start()
            for copy in copies:
                copy.wait()
        from_core.start()
        from_core.wait_send()

    products = inner[...]
    i = lax.broadcasted_iota(jnp.int32, (every, every), 0)
    j = lax.broadcasted_iota(jnp.int32, (every, every), 1)
    norms = jnp.where(i == j, products, 0.0)
    distance = (
        jnp.sum(norms, axis=1, keepdims=True)
        + jnp.sum(norms, axis=0, keepdims=True)
        - 2.0 * products
    )
    inner[...] = jnp.exp(-distance * inv_band)
    near_rows = rows_of(hi * 2 * rows, 2 * rows)
    far_rows = rows_of((1 - hi) * 2 * rows, 2 * rows)
    near_cols = cols_of(hi * 2 * rows, 2 * rows)

    def dot(left, right):
        return jnp.dot(left, right, precision=HIGHEST, preferred_element_type=jnp.float32)

    s_swap.wait()
    s_keep.wait()
    last = step_cols * MAIN_PARTS
    last_cols = pl.ds(last, step_cols)
    product[...] = dot(inner[far_rows, near_cols], s_all[near_rows, last_cols])
    far_copies = [
        send(product.at[pl.ds(slot * rows, rows)], far.at[lo], (far_send.at[slot], far_recv.at[lo]), across[slot])
        for slot in range(2)
    ]
    @pl.when(lo == 1)
    def _():
        far_copies[0].start()
        far_copies[1].start()

    @pl.when(lo == 0)
    def _():
        far_copies[1].start()
        far_copies[0].start()


    step_size = step_ref[0, 0]
    pull = 2.0 * inv_band * jnp.sum(inner[near_rows, :], axis=1, keepdims=True)
    loads[3].wait()
    x_swap.wait()

    def out_cols(u):
        return cols_of(half * lo + step_cols * u, step_cols)

    def out_swap(u):
        return send(
            result.at[rows_of((1 - lo) * rows, rows), cols_of(step_cols * u, step_cols)],
            moved.at[:, out_cols(u)],
            (out_send.at[u], out_recv.at[u]),
            sibling,
        )

    def finish(u, attracted):
        cols = cols_of(step_cols * u, step_cols)
        x = x_chip[:, cols]
        result[:, cols] = x + step_size * ((attracted + pull * x) * (1.0 / every))
        out_swap(u).start()
        moved[:, out_cols(u)] = result[rows_of(lo * rows, rows), cols]

    finish(MAIN_PARTS, dot(inner[near_rows, near_cols], s_all[near_rows, last_cols]))

    @pl.loop(0, MAIN_PARTS)
    def _(u):
        for sem in range(2):
            step_recv(sem, u).wait()
        finish(u, dot(inner[near_rows, :], s_all[:, cols_of(step_cols * u, step_cols)]))

    @pl.loop(0, MAIN_PARTS)
    def _(u):
        for slot in range(2):
            step_copy(slot, u).wait_send()

    @pl.loop(0, GRAM_PARTS)
    def _(c):
        for slot in range(3):
            gram_copy(slot, c).wait_send()

    @pl.loop(0, STEP_PARTS)
    def _(u):
        out_swap(u).wait()

    for slot in range(2):
        pltpu.make_async_copy(far.at[slot], far.at[slot], far_recv.at[slot]).wait()
        cols = pl.ds(half * slot + last, step_cols)
        moved[:, cols] = moved[:, cols] + step_size * (far[slot] * (1.0 / every))
    for copy in far_copies:
        copy.wait_send()


def on_device(dims, width, step_size, particles, gradients):
    rows, cells, nx, nz = dims
    every, half = 4 * rows, cells // 2
    n_x = every // nx
    n_z = n_x // nz
    f32 = jnp.float32
    sem = pltpu.SemaphoreType.DMA
    messages = 5 + 2 * (nx - 1) + 2 * (nz - 1)
    return pl.pallas_call(
        functools.partial(kernel, dims),
        out_shape=pltpu.VMEM((rows, cells), f32),
        in_specs=[pl.BlockSpec(memory_space=pltpu.HBM)] * 4,
        out_specs=pl.BlockSpec(memory_space=pltpu.VMEM),
        scratch_shapes=[
            pltpu.VMEM((rows, cells), f32),
            pltpu.VMEM((rows, cells), f32),
            pltpu.VMEM((every, cells // 4), f32),
            pltpu.VMEM((2 * rows, half), f32),
            pltpu.VMEM((every, half), f32),
            pltpu.VMEM((2 * rows, half), f32),
            pltpu.VMEM((2 * rows, half // STEP_PARTS), f32),
            pltpu.VMEM((2, rows, half // STEP_PARTS), f32),
            pltpu.VMEM((every, every), f32),
            pltpu.VMEM((every, every), f32),
            pltpu.VMEM((nx, n_x, every), f32),
            pltpu.VMEM((nz, n_z, every), f32),
            pltpu.VMEM((3, n_z // 2, every), f32),
            pltpu.VMEM((every, every), f32),
            pltpu.SMEM((1, 1), f32),
            pltpu.SMEM((1, 1), f32),
            pltpu.SemaphoreType.REGULAR,
            sem((7,)),
            sem((3, GRAM_PARTS)),
            sem((3, GRAM_PARTS)),
            sem((2,)),
            sem((2,)),
            sem((2, STEP_PARTS)),
            sem((2, STEP_PARTS)),
            sem((2, messages)),
            sem((STEP_PARTS,)),
            sem((STEP_PARTS,)),
            sem((2,)),
            sem((2,)),
        ],
        compiler_params=pltpu.CompilerParams(
            collective_id=0, has_side_effects=True, vmem_limit_bytes=52 * 2**20
        ),
        cost_estimate=pl.CostEstimate(
            flops=4 * every * every * cells // 4,
            bytes_accessed=5 * 4 * rows * cells,
            transcendentals=2 * rows * every,
        ),
    )(
        width.reshape(1, 1),
        step_size.reshape(1, 1),
        particles,
        gradients,
    )


def solution(mesh):
    def step(particles, gradients, width, step_size):
        rows, cells = particles.shape
        nz = NZ if mesh.shape["cell"] == NX * NYH * NZ else 1
        nx = mesh.shape["cell"] // NYH // nz
        return on_device((rows, cells, nx, nz), width, step_size, particles, gradients)

    in_specs = (P("dom", "cell"), P("dom", "cell"), P(), P())
    out_specs = P("dom", "cell")
    return jax.shard_map(step, mesh=mesh, in_specs=in_specs, out_specs=out_specs, check_vma=False)
```

```python
import functools

import jax
import jax.numpy as jnp
from jax import lax
from jax.experimental import pallas as pl
from jax.experimental.pallas import tpu as pltpu
from jax.sharding import PartitionSpec as P

MESH = pl.DeviceIdType.MESH
HIGHEST = lax.Precision.HIGHEST
NX, NYH, NZ = 4, 2, 4
GRAM_PARTS = 4
STEP_PARTS = 8
MAIN_PARTS = STEP_PARTS - 1
EARLY_PARTS = 3


def kernel(
    dims,
    width_hbm,
    step_hbm,
    particles,
    gradients,
    moved,
    x_own,
    s_own,
    x_gram,
    x_chip,
    s_all,
    result,
    product,
    far,
    part,
    sum_core,
    sum_x,
    sum_z,
    sum_y,
    inner,
    width_ref,
    step_ref,
    ready,
    load_sem,
    x_send,
    x_recv,
    xc_sem,
    ss_sem,
    s_send,
    s_recv,
    red_sem,
    out_send,
    out_recv,
    far_send,
    far_recv,
):
    rows, cells, nx, nz = dims
    every = 4 * rows
    half, quarter = cells // 2, cells // 4
    gram_cols, step_cols = quarter // GRAM_PARTS, half // STEP_PARTS
    dom, cell = lax.axis_index("dom"), lax.axis_index("cell")
    hi, lo = dom // 2, lax.rem(dom, 2)
    cx, cy, cz = cell // (NYH * nz), lax.rem(cell // nz, NYH), lax.rem(cell, nz)

    def cell_of(x, y, z):
        return (x * NYH + y) * nz + z

    sibling = (hi * 2 + 1 - lo, cell)
    across = [((1 - hi) * 2, cell), ((1 - hi) * 2 + 1, cell)]
    along_x = [lax.rem(cx + d, nx) for d in range(1, nx)]
    along_z = [lax.rem(cz + d, nz) for d in range(1, nz)]
    x_peers = [(dom, cell_of(x, cy, cz)) for x in along_x]
    z_peers = [(dom, cell_of(cx, cy, z)) for z in along_z]
    y_near = ((1 - hi) * 2 + lo, cell_of(cx, 1 - cy, cz))
    y_pair = ((1 - hi) * 2 + lo, cell)

    def send(src, dst, sems, to):
        return pltpu.make_async_remote_copy(
            src_ref=src,
            dst_ref=dst,
            send_sem=sems[0],
            recv_sem=sems[1],
            device_id=to,
            device_id_type=MESH,
        )

    def rows_of(index, count):
        return pl.ds(pl.multiple_of(index, count), count)

    def cols_of(index, count):
        return pl.ds(pl.multiple_of(index, count), count)

    def signal(sem, to):
        pl.semaphore_signal(sem, inc=1, device_id=to, device_id_type=MESH)

    cross_peers = [*x_peers, *z_peers, y_near]
    barrier = pltpu.get_barrier_semaphore()
    signal(barrier, y_pair)

    @pl.when(lo == 0)
    def _():
        for peer in cross_peers:
            signal(barrier, peer)

    my_rows = rows_of(dom * rows, rows)
    loads = [
        pltpu.make_async_copy(particles, x_own, load_sem.at[0]),
        pltpu.make_async_copy(gradients, s_own, load_sem.at[1]),
        pltpu.make_async_copy(
            particles.at[:, cols_of(half * lo + quarter * hi, quarter)],
            x_gram.at[my_rows],
            load_sem.at[2],
        ),
        pltpu.make_async_copy(
            particles.at[:, cols_of(half * lo, half)],
            x_chip.at[rows_of(lo * rows, rows)],
            load_sem.at[3],
        ),
        pltpu.make_async_copy(width_hbm, width_ref, load_sem.at[5]),
        pltpu.make_async_copy(step_hbm, step_ref, load_sem.at[6]),
    ]
    def gram_copy(slot, c):
        to = (across + [sibling])[slot]
        to_hi, to_lo = (hi, 1 - lo) if slot == 2 else (1 - hi, slot)
        start = half * to_lo + quarter * to_hi + gram_cols * c
        sem = lo if slot < 2 else 2
        return pltpu.make_async_remote_copy(
            src_ref=particles.at[:, cols_of(start, gram_cols)],
            dst_ref=x_gram.at[my_rows, cols_of(gram_cols * c, gram_cols)],
            send_sem=x_send.at[slot, c],
            recv_sem=x_recv.at[sem, c],
            device_id=to,
            device_id_type=MESH,
        )

    def gram_recv(sem, c):
        block = x_gram.at[pl.ds(0, rows), cols_of(gram_cols * c, gram_cols)]
        return pltpu.make_async_copy(block, block, x_recv.at[sem, c])

    @pl.when(lo == 1)
    def _():
        pl.semaphore_wait(barrier, 1)
        signal(barrier, sibling)
        for c in range(GRAM_PARTS):
            gram_copy(1, c).start()
        pl.semaphore_wait(ready, 1)

    @pl.when(lo == 0)
    def _():
        pl.semaphore_wait(barrier, 2 + len(cross_peers))
        signal(ready, sibling)
        for c in range(GRAM_PARTS):
            gram_copy(1, c).start()

    for c in range(GRAM_PARTS):
        gram_copy(0, c).start()
        gram_copy(2, c).start()
    for load in loads:
        load.start()
    x_swap = send(
        particles.at[:, cols_of(half * (1 - lo), half)],
        x_chip.at[rows_of(lo * rows, rows)],
        (xc_sem.at[0], xc_sem.at[1]),
        sibling,
    )
    x_swap.start()

    loads[4].wait()
    loads[5].wait()
    inv_band = 1.0 / width_ref[0, 0]
    loads[0].wait()
    loads[1].wait()

    @pl.loop(0, STEP_PARTS * 2)
    def _(u):
        cols = cols_of(u * step_cols, step_cols)
        s_own[:, cols] = s_own[:, cols] - 2.0 * inv_band * x_own[:, cols]

    def step_copy(slot, u):
        return pltpu.make_async_remote_copy(
            src_ref=s_own.at[:, cols_of(half * slot + step_cols * u, step_cols)],
            dst_ref=s_all.at[my_rows, cols_of(step_cols * u, step_cols)],
            send_sem=s_send.at[slot, u],
            recv_sem=s_recv.at[lo, u],
            device_id=across[slot],
            device_id_type=MESH,
        )

    def step_recv(sem, u):
        block = s_all.at[pl.ds(0, rows), cols_of(step_cols * u, step_cols)]
        return pltpu.make_async_copy(block, block, s_recv.at[sem, u])

    @pl.loop(0, EARLY_PARTS)
    def _(u):
        for slot in range(2):
            step_copy(slot, u).start()

    s_swap = send(
        s_own.at[:, cols_of(half * (1 - lo), half)],
        s_all.at[my_rows],
        (ss_sem.at[0], ss_sem.at[1]),
        sibling,
    )
    s_swap.start()
    s_keep = pltpu.make_async_copy(
        s_own.at[:, cols_of(half * lo, half)], s_all.at[my_rows], load_sem.at[4]
    )
    s_keep.start()

    loads[2].wait()
    part[...] = jnp.zeros_like(part)

    @pl.loop(0, GRAM_PARTS)
    def _(c):
        for sem in range(3):
            if sem == 2:
                gram_recv(2, c).wait()
            else:
                gram_recv(sem, c).wait()
        block = x_gram[:, cols_of(gram_cols * c, gram_cols)]
        part[...] += lax.dot_general(
            block,
            block,
            (((1,), (1,)), ((), ())),
            precision=HIGHEST,
            preferred_element_type=jnp.float32,
        )

    n_x, n_z, n_y = every // nx, every // nx // nz, every // nx // nz // 2
    count = [0]

    def sems():
        k = count[0]
        count[0] += 1
        return red_sem.at[0, k], red_sem.at[1, k]

    def later_parts():
        @pl.loop(EARLY_PARTS, MAIN_PARTS)
        def _(u):
            for slot in range(2):
                step_copy(slot, u).start()

    to_core = send(part, sum_core, sems(), sibling)
    from_core = send(inner, inner, sems(), sibling)

    @pl.when(lo == 1)
    def _():
        to_core.start()
        to_core.wait_send()
        later_parts()
        from_core.wait_recv()

    @pl.when(lo == 0)
    def _():
        to_core.wait_recv()
        sum_core[...] += part[...]
        copies = [
            send(sum_core.at[rows_of(x * n_x, n_x)], sum_x.at[d], sems(), peer)
            for d, (x, peer) in enumerate(zip(along_x, x_peers, strict=True))
        ]
        for copy in copies:
            copy.start()
        total = sum_core[rows_of(cx * n_x, n_x), :]
        for d, copy in enumerate(copies):
            copy.wait()
            total = total + sum_x[d]
        sum_x[nx - 1] = total

        copies = [
            send(sum_x.at[nx - 1, rows_of(z * n_z, n_z)], sum_z.at[d], sems(), peer)
            for d, (z, peer) in enumerate(zip(along_z, z_peers, strict=True))
        ]
        for copy in copies:
            copy.start()
        total = sum_x[nx - 1, rows_of(cz * n_z, n_z), :]
        for d, copy in enumerate(copies):
            copy.wait()
            total = total + sum_z[d]
        sum_z[nz - 1] = total

        swap = send(sum_z.at[nz - 1, rows_of((1 - cy) * n_y, n_y)], sum_y.at[0], sems(), y_near)
        swap.start()
        swap.wait()
        sum_y[1] = sum_y[0] + sum_z[nz - 1, rows_of(cy * n_y, n_y), :]
        swap = send(sum_y.at[1], sum_y.at[2], sems(), y_pair)
        swap.start()
        later_parts()
        swap.wait()
        y_rows = rows_of(cx * n_x + cz * n_z + cy * n_y, n_y)
        z_rows = rows_of(cx * n_x + cz * n_z, n_z)
        x_rows = rows_of(cx * n_x, n_x)
        inner[y_rows, :] = sum_y[1] + sum_y[2]
        for block, peers in ((y_rows, [y_near]), (z_rows, z_peers), (x_rows, x_peers)):
            copies = [send(inner.at[block], inner.at[block], sems(), peer) for peer in peers]
            for copy in copies:
                copy.start()
            for copy in copies:
                copy.wait()
        from_core.start()
        from_core.wait_send()

    products = inner[...]
    i = lax.broadcasted_iota(jnp.int32, (every, every), 0)
    j = lax.broadcasted_iota(jnp.int32, (every, every), 1)
    norms = jnp.where(i == j, products, 0.0)
    distance = (
        jnp.sum(norms, axis=1, keepdims=True)
        + jnp.sum(norms, axis=0, keepdims=True)
        - 2.0 * products
    )
    inner[...] = jnp.exp(-distance * inv_band)
    near_rows = rows_of(hi * 2 * rows, 2 * rows)
    far_rows = rows_of((1 - hi) * 2 * rows, 2 * rows)
    near_cols = cols_of(hi * 2 * rows, 2 * rows)

    def dot(left, right):
        return jnp.dot(left, right, precision=HIGHEST, preferred_element_type=jnp.float32)

    s_swap.wait()
    s_keep.wait()
    last = step_cols * MAIN_PARTS
    last_cols = pl.ds(last, step_cols)
    product[...] = dot(inner[far_rows, near_cols], s_all[near_rows, last_cols])
    far_copies = [
        send(product.at[pl.ds(slot * rows, rows)], far.at[lo], (far_send.at[slot], far_recv.at[lo]), across[slot])
        for slot in range(2)
    ]
    @pl.when(lo == 1)
    def _():
        far_copies[0].start()
        far_copies[1].start()

    @pl.when(lo == 0)
    def _():
        far_copies[1].start()
        far_copies[0].start()


    step_size = step_ref[0, 0]
    pull = 2.0 * inv_band * jnp.sum(inner[near_rows, :], axis=1, keepdims=True)
    loads[3].wait()
    x_swap.wait()

    def out_cols(u):
        return cols_of(half * lo + step_cols * u, step_cols)

    def out_swap(u):
        return send(
            result.at[rows_of((1 - lo) * rows, rows), cols_of(step_cols * u, step_cols)],
            moved.at[:, out_cols(u)],
            (out_send.at[u], out_recv.at[u]),
            sibling,
        )

    def finish(u, attracted):
        cols = cols_of(step_cols * u, step_cols)
        x = x_chip[:, cols]
        result[:, cols] = x + step_size * ((attracted + pull * x) * (1.0 / every))
        out_swap(u).start()
        moved[:, out_cols(u)] = result[rows_of(lo * rows, rows), cols]

    finish(MAIN_PARTS, dot(inner[near_rows, near_cols], s_all[near_rows, last_cols]))

    @pl.loop(0, MAIN_PARTS)
    def _(u):
        for sem in range(2):
            step_recv(sem, u).wait()
        finish(u, dot(inner[near_rows, :], s_all[:, cols_of(step_cols * u, step_cols)]))

    @pl.loop(0, MAIN_PARTS)
    def _(u):
        for slot in range(2):
            step_copy(slot, u).wait_send()

    @pl.loop(0, GRAM_PARTS)
    def _(c):
        for slot in range(3):
            gram_copy(slot, c).wait_send()

    @pl.loop(0, STEP_PARTS)
    def _(u):
        out_swap(u).wait()

    for slot in range(2):
        pltpu.make_async_copy(far.at[slot], far.at[slot], far_recv.at[slot]).wait()
        cols = pl.ds(half * slot + last, step_cols)
        moved[:, cols] = moved[:, cols] + step_size * (far[slot] * (1.0 / every))
    for copy in far_copies:
        copy.wait_send()


def on_device(dims, width, step_size, particles, gradients):
    rows, cells, nx, nz = dims
    every, half = 4 * rows, cells // 2
    n_x = every // nx
    n_z = n_x // nz
    f32 = jnp.float32
    sem = pltpu.SemaphoreType.DMA
    messages = 5 + 2 * (nx - 1) + 2 * (nz - 1)
    return pl.pallas_call(
        functools.partial(kernel, dims),
        out_shape=pltpu.VMEM((rows, cells), f32),
        in_specs=[pl.BlockSpec(memory_space=pltpu.HBM)] * 4,
        out_specs=pl.BlockSpec(memory_space=pltpu.VMEM),
        scratch_shapes=[
            pltpu.VMEM((rows, cells), f32),
            pltpu.VMEM((rows, cells), f32),
            pltpu.VMEM((every, cells // 4), f32),
            pltpu.VMEM((2 * rows, half), f32),
            pltpu.VMEM((every, half), f32),
            pltpu.VMEM((2 * rows, half), f32),
            pltpu.VMEM((2 * rows, half // STEP_PARTS), f32),
            pltpu.VMEM((2, rows, half // STEP_PARTS), f32),
            pltpu.VMEM((every, every), f32),
            pltpu.VMEM((every, every), f32),
            pltpu.VMEM((nx, n_x, every), f32),
            pltpu.VMEM((nz, n_z, every), f32),
            pltpu.VMEM((3, n_z // 2, every), f32),
            pltpu.VMEM((every, every), f32),
            pltpu.SMEM((1, 1), f32),
            pltpu.SMEM((1, 1), f32),
            pltpu.SemaphoreType.REGULAR,
            sem((7,)),
            sem((3, GRAM_PARTS)),
            sem((3, GRAM_PARTS)),
            sem((2,)),
            sem((2,)),
            sem((2, STEP_PARTS)),
            sem((2, STEP_PARTS)),
            sem((2, messages)),
            sem((STEP_PARTS,)),
            sem((STEP_PARTS,)),
            sem((2,)),
            sem((2,)),
        ],
        compiler_params=pltpu.CompilerParams(
            collective_id=0, has_side_effects=True, vmem_limit_bytes=52 * 2**20
        ),
        cost_estimate=pl.CostEstimate(
            flops=4 * every * every * cells // 4,
            bytes_accessed=5 * 4 * rows * cells,
            transcendentals=2 * rows * every,
        ),
    )(
        width.reshape(1, 1),
        step_size.reshape(1, 1),
        particles,
        gradients,
    )


def solution(mesh):
    def step(particles, gradients, width, step_size):
        rows, cells = particles.shape
        nz = NZ if mesh.shape["cell"] == NX * NYH * NZ else 1
        nx = mesh.shape["cell"] // NYH // nz
        return on_device((rows, cells, nx, nz), width, step_size, particles, gradients)

    in_specs = (P("dom", "cell"), P("dom", "cell"), P(), P())
    out_specs = P("dom", "cell")
    return jax.shard_map(step, mesh=mesh, in_specs=in_specs, out_specs=out_specs, check_vma=False)
```

```python
import functools

import jax
import jax.numpy as jnp
from jax import lax
from jax.experimental import pallas as pl
from jax.experimental.pallas import tpu as pltpu
from jax.sharding import PartitionSpec as P

MESH = pl.DeviceIdType.MESH
HIGHEST = lax.Precision.HIGHEST
NX, NYH, NZ = 4, 2, 4
GRAM_PARTS = 4
STEP_PARTS = 8
MAIN_PARTS = STEP_PARTS - 1
EARLY_PARTS = 3


def kernel(
    dims,
    width_hbm,
    step_hbm,
    particles,
    gradients,
    moved,
    x_own,
    s_own,
    x_gram,
    x_chip,
    s_all,
    result,
    product,
    far,
    part,
    sum_core,
    sum_x,
    sum_z,
    sum_y,
    inner,
    width_ref,
    step_ref,
    ready,
    load_sem,
    x_send,
    x_recv,
    xc_sem,
    ss_sem,
    s_send,
    s_recv,
    red_sem,
    out_send,
    out_recv,
    far_send,
    far_recv,
):
    rows, cells, nx, nz = dims
    every = 4 * rows
    half, quarter = cells // 2, cells // 4
    gram_cols, step_cols = quarter // GRAM_PARTS, half // STEP_PARTS
    dom, cell = lax.axis_index("dom"), lax.axis_index("cell")
    hi, lo = dom // 2, lax.rem(dom, 2)
    cx, cy, cz = cell // (NYH * nz), lax.rem(cell // nz, NYH), lax.rem(cell, nz)

    def cell_of(x, y, z):
        return (x * NYH + y) * nz + z

    sibling = (hi * 2 + 1 - lo, cell)
    across = [((1 - hi) * 2, cell), ((1 - hi) * 2 + 1, cell)]
    along_x = [lax.rem(cx + d, nx) for d in range(1, nx)]
    along_z = [lax.rem(cz + d, nz) for d in range(1, nz)]
    x_peers = [(dom, cell_of(x, cy, cz)) for x in along_x]
    z_peers = [(dom, cell_of(cx, cy, z)) for z in along_z]
    y_near = ((1 - hi) * 2 + lo, cell_of(cx, 1 - cy, cz))
    y_pair = ((1 - hi) * 2 + lo, cell)

    def send(src, dst, sems, to):
        return pltpu.make_async_remote_copy(
            src_ref=src,
            dst_ref=dst,
            send_sem=sems[0],
            recv_sem=sems[1],
            device_id=to,
            device_id_type=MESH,
        )

    def rows_of(index, count):
        return pl.ds(pl.multiple_of(index, count), count)

    def cols_of(index, count):
        return pl.ds(pl.multiple_of(index, count), count)

    def signal(sem, to):
        pl.semaphore_signal(sem, inc=1, device_id=to, device_id_type=MESH)

    cross_peers = [*x_peers, *z_peers, y_near]
    barrier = pltpu.get_barrier_semaphore()
    signal(barrier, y_pair)

    @pl.when(lo == 0)
    def _():
        for peer in cross_peers:
            signal(barrier, peer)

    my_rows = rows_of(dom * rows, rows)
    loads = [
        pltpu.make_async_copy(particles, x_own, load_sem.at[0]),
        pltpu.make_async_copy(gradients, s_own, load_sem.at[1]),
        pltpu.make_async_copy(
            particles.at[:, cols_of(half * lo + quarter * hi, quarter)],
            x_gram.at[my_rows],
            load_sem.at[2],
        ),
        pltpu.make_async_copy(
            particles.at[:, cols_of(half * lo, half)],
            x_chip.at[rows_of(lo * rows, rows)],
            load_sem.at[3],
        ),
        pltpu.make_async_copy(width_hbm, width_ref, load_sem.at[5]),
        pltpu.make_async_copy(step_hbm, step_ref, load_sem.at[6]),
    ]
    def gram_copy(slot, c):
        to = (across + [sibling])[slot]
        to_hi, to_lo = (hi, 1 - lo) if slot == 2 else (1 - hi, slot)
        start = half * to_lo + quarter * to_hi + gram_cols * c
        sem = lo if slot < 2 else 2
        return pltpu.make_async_remote_copy(
            src_ref=particles.at[:, cols_of(start, gram_cols)],
            dst_ref=x_gram.at[my_rows, cols_of(gram_cols * c, gram_cols)],
            send_sem=x_send.at[slot, c],
            recv_sem=x_recv.at[sem, c],
            device_id=to,
            device_id_type=MESH,
        )

    def gram_recv(sem, c):
        block = x_gram.at[pl.ds(0, rows), cols_of(gram_cols * c, gram_cols)]
        return pltpu.make_async_copy(block, block, x_recv.at[sem, c])

    @pl.when(lo == 1)
    def _():
        pl.semaphore_wait(barrier, 1)
        signal(barrier, sibling)
        for c in range(GRAM_PARTS):
            gram_copy(1, c).start()
        pl.semaphore_wait(ready, 1)

    @pl.when(lo == 0)
    def _():
        pl.semaphore_wait(barrier, 2 + len(cross_peers))
        signal(ready, sibling)
        for c in range(GRAM_PARTS):
            gram_copy(1, c).start()

    for c in range(GRAM_PARTS):
        gram_copy(0, c).start()
        gram_copy(2, c).start()
    for load in loads:
        load.start()
    x_swap = send(
        particles.at[:, cols_of(half * (1 - lo), half)],
        x_chip.at[rows_of(lo * rows, rows)],
        (xc_sem.at[0], xc_sem.at[1]),
        sibling,
    )
    x_swap.start()

    loads[4].wait()
    loads[5].wait()
    inv_band = 1.0 / width_ref[0, 0]
    loads[0].wait()
    loads[1].wait()

    @pl.loop(0, STEP_PARTS * 2)
    def _(u):
        cols = cols_of(u * step_cols, step_cols)
        s_own[:, cols] = s_own[:, cols] - 2.0 * inv_band * x_own[:, cols]

    def step_copy(slot, u):
        return pltpu.make_async_remote_copy(
            src_ref=s_own.at[:, cols_of(half * slot + step_cols * u, step_cols)],
            dst_ref=s_all.at[my_rows, cols_of(step_cols * u, step_cols)],
            send_sem=s_send.at[slot, u],
            recv_sem=s_recv.at[lo, u],
            device_id=across[slot],
            device_id_type=MESH,
        )

    def step_recv(sem, u):
        block = s_all.at[pl.ds(0, rows), cols_of(step_cols * u, step_cols)]
        return pltpu.make_async_copy(block, block, s_recv.at[sem, u])

    @pl.loop(0, EARLY_PARTS)
    def _(u):
        for slot in range(2):
            step_copy(slot, u).start()

    s_swap = send(
        s_own.at[:, cols_of(half * (1 - lo), half)],
        s_all.at[my_rows],
        (ss_sem.at[0], ss_sem.at[1]),
        sibling,
    )
    s_swap.start()
    s_keep = pltpu.make_async_copy(
        s_own.at[:, cols_of(half * lo, half)], s_all.at[my_rows], load_sem.at[4]
    )
    s_keep.start()

    loads[2].wait()
    part[...] = jnp.zeros_like(part)

    @pl.loop(0, GRAM_PARTS)
    def _(c):
        for sem in range(3):
            gram_recv(sem, c).wait()
        block = x_gram[:, cols_of(gram_cols * c, gram_cols)]
        part[...] += lax.dot_general(
            block,
            block,
            (((1,), (1,)), ((), ())),
            precision=HIGHEST,
            preferred_element_type=jnp.float32,
        )

    n_x, n_z, n_y = every // nx, every // nx // nz, every // nx // nz // 2
    count = [0]

    def sems():
        k = count[0]
        count[0] += 1
        return red_sem.at[0, k], red_sem.at[1, k]

    def later_parts():
        @pl.loop(EARLY_PARTS, MAIN_PARTS)
        def _(u):
            for slot in range(2):
                step_copy(slot, u).start()

    to_core = send(part, sum_core, sems(), sibling)
    from_core = send(inner, inner, sems(), sibling)

    @pl.when(lo == 1)
    def _():
        to_core.start()
        to_core.wait_send()
        later_parts()
        from_core.wait_recv()

    @pl.when(lo == 0)
    def _():
        to_core.wait_recv()
        sum_core[...] += part[...]
        copies = [
            send(sum_core.at[rows_of(x * n_x, n_x)], sum_x.at[d], sems(), peer)
            for d, (x, peer) in enumerate(zip(along_x, x_peers, strict=True))
        ]
        for copy in copies:
            copy.start()
        total = sum_core[rows_of(cx * n_x, n_x), :]
        for d, copy in enumerate(copies):
            copy.wait()
            total = total + sum_x[d]
        sum_x[nx - 1] = total

        copies = [
            send(sum_x.at[nx - 1, rows_of(z * n_z, n_z)], sum_z.at[d], sems(), peer)
            for d, (z, peer) in enumerate(zip(along_z, z_peers, strict=True))
        ]
        for copy in copies:
            copy.start()
        total = sum_x[nx - 1, rows_of(cz * n_z, n_z), :]
        for d, copy in enumerate(copies):
            copy.wait()
            total = total + sum_z[d]
        sum_z[nz - 1] = total

        swap = send(sum_z.at[nz - 1, rows_of((1 - cy) * n_y, n_y)], sum_y.at[0], sems(), y_near)
        swap.start()
        swap.wait()
        sum_y[1] = sum_y[0] + sum_z[nz - 1, rows_of(cy * n_y, n_y), :]
        swap = send(sum_y.at[1], sum_y.at[2], sems(), y_pair)
        swap.start()
        later_parts()
        swap.wait()
        y_rows = rows_of(cx * n_x + cz * n_z + cy * n_y, n_y)
        z_rows = rows_of(cx * n_x + cz * n_z, n_z)
        x_rows = rows_of(cx * n_x, n_x)
        inner[y_rows, :] = sum_y[1] + sum_y[2]
        for block, peers in ((y_rows, [y_near]), (z_rows, z_peers), (x_rows, x_peers)):
            copies = [send(inner.at[block], inner.at[block], sems(), peer) for peer in peers]
            for copy in copies:
                copy.start()
            for copy in copies:
                copy.wait()
        from_core.start()
        from_core.wait_send()

    products = inner[...]
    i = lax.broadcasted_iota(jnp.int32, (every, every), 0)
    j = lax.broadcasted_iota(jnp.int32, (every, every), 1)
    norms = jnp.where(i == j, products, 0.0)
    distance = (
        jnp.sum(norms, axis=1, keepdims=True)
        + jnp.sum(norms, axis=0, keepdims=True)
        - 2.0 * products
    )
    inner[...] = jnp.exp(-distance * inv_band)
    near_rows = rows_of(hi * 2 * rows, 2 * rows)
    far_rows = rows_of((1 - hi) * 2 * rows, 2 * rows)
    near_cols = cols_of(hi * 2 * rows, 2 * rows)

    def dot(left, right):
        return jnp.dot(left, right, precision=HIGHEST, preferred_element_type=jnp.float32)

    s_swap.wait()
    s_keep.wait()
    last = step_cols * MAIN_PARTS
    last_cols = pl.ds(last, step_cols)
    product[...] = dot(inner[far_rows, near_cols], s_all[near_rows, last_cols])
    far_copies = [
        send(product.at[pl.ds(slot * rows, rows)], far.at[lo], (far_send.at[slot], far_recv.at[lo]), across[slot])
        for slot in range(2)
    ]
    @pl.when(lo == 1)
    def _():
        far_copies[0].start()
        far_copies[1].start()

    @pl.when(lo == 0)
    def _():
        far_copies[1].start()
        far_copies[0].start()


    step_size = step_ref[0, 0]
    pull = 2.0 * inv_band * jnp.sum(inner[near_rows, :], axis=1, keepdims=True)
    loads[3].wait()
    x_swap.wait()

    def out_cols(u):
        return cols_of(half * lo + step_cols * u, step_cols)

    def out_swap(u):
        return send(
            result.at[rows_of((1 - lo) * rows, rows), cols_of(step_cols * u, step_cols)],
            moved.at[:, out_cols(u)],
            (out_send.at[u], out_recv.at[u]),
            sibling,
        )

    def finish(u, attracted):
        cols = cols_of(step_cols * u, step_cols)
        x = x_chip[:, cols]
        result[:, cols] = x + step_size * ((attracted + pull * x) * (1.0 / every))
        out_swap(u).start()
        moved[:, out_cols(u)] = result[rows_of(lo * rows, rows), cols]

    finish(MAIN_PARTS, dot(inner[near_rows, near_cols], s_all[near_rows, last_cols]))

    @pl.loop(0, GRAM_PARTS)
    def _(c):
        for slot in range(3):
            gram_copy(slot, c).wait_send()

    def leave(u):
        for slot in range(2):
            step_copy(slot, u).wait_send()
        out_swap(u).wait()

    @pl.loop(0, MAIN_PARTS)
    def _(u):
        for sem in range(2):
            step_recv(sem, u).wait()
        finish(u, dot(inner[near_rows, :], s_all[:, cols_of(step_cols * u, step_cols)]))

        @pl.when(u > 0)
        def _():
            leave(u - 1)

    leave(MAIN_PARTS - 1)
    out_swap(MAIN_PARTS).wait()
    for slot in (1, 0):
        pltpu.make_async_copy(far.at[slot], far.at[slot], far_recv.at[slot]).wait()
        cols = pl.ds(half * slot + last, step_cols)
        moved[:, cols] = moved[:, cols] + step_size * (far[slot] * (1.0 / every))
    for copy in far_copies:
        copy.wait_send()


def on_device(dims, width, step_size, particles, gradients):
    rows, cells, nx, nz = dims
    every, half = 4 * rows, cells // 2
    n_x = every // nx
    n_z = n_x // nz
    f32 = jnp.float32
    sem = pltpu.SemaphoreType.DMA
    messages = 5 + 2 * (nx - 1) + 2 * (nz - 1)
    return pl.pallas_call(
        functools.partial(kernel, dims),
        out_shape=pltpu.VMEM((rows, cells), f32),
        in_specs=[pl.BlockSpec(memory_space=pltpu.HBM)] * 4,
        out_specs=pl.BlockSpec(memory_space=pltpu.VMEM),
        scratch_shapes=[
            pltpu.VMEM((rows, cells), f32),
            pltpu.VMEM((rows, cells), f32),
            pltpu.VMEM((every, cells // 4), f32),
            pltpu.VMEM((2 * rows, half), f32),
            pltpu.VMEM((every, half), f32),
            pltpu.VMEM((2 * rows, half), f32),
            pltpu.VMEM((2 * rows, half // STEP_PARTS), f32),
            pltpu.VMEM((2, rows, half // STEP_PARTS), f32),
            pltpu.VMEM((every, every), f32),
            pltpu.VMEM((every, every), f32),
            pltpu.VMEM((nx, n_x, every), f32),
            pltpu.VMEM((nz, n_z, every), f32),
            pltpu.VMEM((3, n_z // 2, every), f32),
            pltpu.VMEM((every, every), f32),
            pltpu.SMEM((1, 1), f32),
            pltpu.SMEM((1, 1), f32),
            pltpu.SemaphoreType.REGULAR,
            sem((7,)),
            sem((3, GRAM_PARTS)),
            sem((3, GRAM_PARTS)),
            sem((2,)),
            sem((2,)),
            sem((2, STEP_PARTS)),
            sem((2, STEP_PARTS)),
            sem((2, messages)),
            sem((STEP_PARTS,)),
            sem((STEP_PARTS,)),
            sem((2,)),
            sem((2,)),
        ],
        compiler_params=pltpu.CompilerParams(
            collective_id=0, has_side_effects=True, vmem_limit_bytes=52 * 2**20
        ),
        cost_estimate=pl.CostEstimate(
            flops=4 * every * every * cells // 4,
            bytes_accessed=5 * 4 * rows * cells,
            transcendentals=2 * rows * every,
        ),
    )(
        width.reshape(1, 1),
        step_size.reshape(1, 1),
        particles,
        gradients,
    )


def solution(mesh):
    def step(particles, gradients, width, step_size):
        rows, cells = particles.shape
        nz = NZ if mesh.shape["cell"] == NX * NYH * NZ else 1
        nx = mesh.shape["cell"] // NYH // nz
        return on_device((rows, cells, nx, nz), width, step_size, particles, gradients)

    in_specs = (P("dom", "cell"), P("dom", "cell"), P(), P())
    out_specs = P("dom", "cell")
    return jax.shard_map(step, mesh=mesh, in_specs=in_specs, out_specs=out_specs, check_vma=False)
```

```python
import functools

import jax
import jax.numpy as jnp
from jax import lax
from jax.experimental import pallas as pl
from jax.experimental.pallas import tpu as pltpu
from jax.sharding import PartitionSpec as P

MESH = pl.DeviceIdType.MESH
HIGHEST = lax.Precision.HIGHEST
NX, NYH, NZ = 4, 2, 4
GRAM_PARTS = 4
STEP_PARTS = 8
LAST_PARTS = 2
MAIN_PARTS = STEP_PARTS - LAST_PARTS
EARLY_PARTS = 3


def kernel(
    dims,
    width_hbm,
    step_hbm,
    particles,
    gradients,
    moved,
    x_own,
    s_own,
    x_gram,
    x_chip,
    s_all,
    result,
    product,
    far,
    part,
    sum_core,
    sum_x,
    sum_z,
    sum_y,
    inner,
    width_ref,
    step_ref,
    ready,
    load_sem,
    x_send,
    x_recv,
    xc_sem,
    ss_sem,
    s_send,
    s_recv,
    red_sem,
    out_send,
    out_recv,
    far_send,
    far_recv,
):
    rows, cells, nx, nz = dims
    every = 4 * rows
    half, quarter = cells // 2, cells // 4
    gram_cols, step_cols = quarter // GRAM_PARTS, half // STEP_PARTS
    dom, cell = lax.axis_index("dom"), lax.axis_index("cell")
    hi, lo = dom // 2, lax.rem(dom, 2)
    cx, cy, cz = cell // (NYH * nz), lax.rem(cell // nz, NYH), lax.rem(cell, nz)

    def cell_of(x, y, z):
        return (x * NYH + y) * nz + z

    sibling = (hi * 2 + 1 - lo, cell)
    across = [((1 - hi) * 2, cell), ((1 - hi) * 2 + 1, cell)]
    along_x = [lax.rem(cx + d, nx) for d in range(1, nx)]
    along_z = [lax.rem(cz + d, nz) for d in range(1, nz)]
    x_peers = [(dom, cell_of(x, cy, cz)) for x in along_x]
    z_peers = [(dom, cell_of(cx, cy, z)) for z in along_z]
    y_near = ((1 - hi) * 2 + lo, cell_of(cx, 1 - cy, cz))
    y_pair = ((1 - hi) * 2 + lo, cell)

    def send(src, dst, sems, to):
        return pltpu.make_async_remote_copy(
            src_ref=src,
            dst_ref=dst,
            send_sem=sems[0],
            recv_sem=sems[1],
            device_id=to,
            device_id_type=MESH,
        )

    def rows_of(index, count):
        return pl.ds(pl.multiple_of(index, count), count)

    def cols_of(index, count):
        return pl.ds(pl.multiple_of(index, count), count)

    def signal(sem, to):
        pl.semaphore_signal(sem, inc=1, device_id=to, device_id_type=MESH)

    cross_peers = [*x_peers, *z_peers, y_near]
    barrier = pltpu.get_barrier_semaphore()
    signal(barrier, y_pair)

    @pl.when(lo == 0)
    def _():
        for peer in cross_peers:
            signal(barrier, peer)

    my_rows = rows_of(dom * rows, rows)
    loads = [
        pltpu.make_async_copy(particles, x_own, load_sem.at[0]),
        pltpu.make_async_copy(gradients, s_own, load_sem.at[1]),
        pltpu.make_async_copy(
            particles.at[:, cols_of(half * lo + quarter * hi, quarter)],
            x_gram.at[my_rows],
            load_sem.at[2],
        ),
        pltpu.make_async_copy(
            particles.at[:, cols_of(half * lo, half)],
            x_chip.at[rows_of(lo * rows, rows)],
            load_sem.at[3],
        ),
        pltpu.make_async_copy(width_hbm, width_ref, load_sem.at[5]),
        pltpu.make_async_copy(step_hbm, step_ref, load_sem.at[6]),
    ]
    def gram_copy(slot, c):
        to = (across + [sibling])[slot]
        to_hi, to_lo = (hi, 1 - lo) if slot == 2 else (1 - hi, slot)
        start = half * to_lo + quarter * to_hi + gram_cols * c
        sem = lo if slot < 2 else 2
        return pltpu.make_async_remote_copy(
            src_ref=particles.at[:, cols_of(start, gram_cols)],
            dst_ref=x_gram.at[my_rows, cols_of(gram_cols * c, gram_cols)],
            send_sem=x_send.at[slot, c],
            recv_sem=x_recv.at[sem, c],
            device_id=to,
            device_id_type=MESH,
        )

    def gram_recv(sem, c):
        block = x_gram.at[pl.ds(0, rows), cols_of(gram_cols * c, gram_cols)]
        return pltpu.make_async_copy(block, block, x_recv.at[sem, c])

    @pl.when(lo == 1)
    def _():
        pl.semaphore_wait(barrier, 1)
        signal(barrier, sibling)
        for c in range(GRAM_PARTS):
            gram_copy(1, c).start()
        pl.semaphore_wait(ready, 1)

    @pl.when(lo == 0)
    def _():
        pl.semaphore_wait(barrier, 2 + len(cross_peers))
        signal(ready, sibling)
        for c in range(GRAM_PARTS):
            gram_copy(1, c).start()

    for c in range(GRAM_PARTS):
        gram_copy(0, c).start()
        gram_copy(2, c).start()
    for load in loads:
        load.start()
    x_swap = send(
        particles.at[:, cols_of(half * (1 - lo), half)],
        x_chip.at[rows_of(lo * rows, rows)],
        (xc_sem.at[0], xc_sem.at[1]),
        sibling,
    )
    x_swap.start()

    loads[4].wait()
    loads[5].wait()
    inv_band = 1.0 / width_ref[0, 0]
    loads[0].wait()
    loads[1].wait()

    @pl.loop(0, STEP_PARTS * 2)
    def _(u):
        cols = cols_of(u * step_cols, step_cols)
        s_own[:, cols] = s_own[:, cols] - 2.0 * inv_band * x_own[:, cols]

    def step_copy(slot, u):
        return pltpu.make_async_remote_copy(
            src_ref=s_own.at[:, cols_of(half * slot + step_cols * u, step_cols)],
            dst_ref=s_all.at[my_rows, cols_of(step_cols * u, step_cols)],
            send_sem=s_send.at[slot, u],
            recv_sem=s_recv.at[lo, u],
            device_id=across[slot],
            device_id_type=MESH,
        )

    def step_recv(sem, u):
        block = s_all.at[pl.ds(0, rows), cols_of(step_cols * u, step_cols)]
        return pltpu.make_async_copy(block, block, s_recv.at[sem, u])

    @pl.loop(0, EARLY_PARTS)
    def _(u):
        for slot in range(2):
            step_copy(slot, u).start()

    s_swap = send(
        s_own.at[:, cols_of(half * (1 - lo), half)],
        s_all.at[my_rows],
        (ss_sem.at[0], ss_sem.at[1]),
        sibling,
    )
    s_swap.start()
    s_keep = pltpu.make_async_copy(
        s_own.at[:, cols_of(half * lo, half)], s_all.at[my_rows], load_sem.at[4]
    )
    s_keep.start()

    loads[2].wait()
    part[...] = jnp.zeros_like(part)

    @pl.loop(0, GRAM_PARTS)
    def _(c):
        for sem in range(3):
            if sem == 2:
                gram_recv(2, c).wait()
            else:
                gram_recv(sem, c).wait()
        block = x_gram[:, cols_of(gram_cols * c, gram_cols)]
        part[...] += lax.dot_general(
            block,
            block,
            (((1,), (1,)), ((), ())),
            precision=HIGHEST,
            preferred_element_type=jnp.float32,
        )

    n_x, n_z, n_y = every // nx, every // nx // nz, every // nx // nz // 2
    count = [0]

    def sems():
        k = count[0]
        count[0] += 1
        return red_sem.at[0, k], red_sem.at[1, k]

    def later_parts():
        @pl.loop(EARLY_PARTS, MAIN_PARTS)
        def _(u):
            for slot in range(2):
                step_copy(slot, u).start()

    to_core = send(part, sum_core, sems(), sibling)
    from_core = send(inner, inner, sems(), sibling)

    @pl.when(lo == 1)
    def _():
        to_core.start()
        to_core.wait_send()
        later_parts()
        from_core.wait_recv()

    @pl.when(lo == 0)
    def _():
        to_core.wait_recv()
        sum_core[...] += part[...]
        copies = [
            send(sum_core.at[rows_of(x * n_x, n_x)], sum_x.at[d], sems(), peer)
            for d, (x, peer) in enumerate(zip(along_x, x_peers, strict=True))
        ]
        for copy in copies:
            copy.start()
        total = sum_core[rows_of(cx * n_x, n_x), :]
        for d, copy in enumerate(copies):
            copy.wait()
            total = total + sum_x[d]
        sum_x[nx - 1] = total

        copies = [
            send(sum_x.at[nx - 1, rows_of(z * n_z, n_z)], sum_z.at[d], sems(), peer)
            for d, (z, peer) in enumerate(zip(along_z, z_peers, strict=True))
        ]
        for copy in copies:
            copy.start()
        total = sum_x[nx - 1, rows_of(cz * n_z, n_z), :]
        for d, copy in enumerate(copies):
            copy.wait()
            total = total + sum_z[d]
        sum_z[nz - 1] = total

        swap = send(sum_z.at[nz - 1, rows_of((1 - cy) * n_y, n_y)], sum_y.at[0], sems(), y_near)
        swap.start()
        swap.wait()
        sum_y[1] = sum_y[0] + sum_z[nz - 1, rows_of(cy * n_y, n_y), :]
        swap = send(sum_y.at[1], sum_y.at[2], sems(), y_pair)
        swap.start()
        later_parts()
        swap.wait()
        y_rows = rows_of(cx * n_x + cz * n_z + cy * n_y, n_y)
        z_rows = rows_of(cx * n_x + cz * n_z, n_z)
        x_rows = rows_of(cx * n_x, n_x)
        inner[y_rows, :] = sum_y[1] + sum_y[2]
        for block, peers in ((y_rows, [y_near]), (z_rows, z_peers), (x_rows, x_peers)):
            copies = [send(inner.at[block], inner.at[block], sems(), peer) for peer in peers]
            for copy in copies:
                copy.start()
            for copy in copies:
                copy.wait()
        from_core.start()
        from_core.wait_send()

    products = inner[...]
    i = lax.broadcasted_iota(jnp.int32, (every, every), 0)
    j = lax.broadcasted_iota(jnp.int32, (every, every), 1)
    norms = jnp.where(i == j, products, 0.0)
    distance = (
        jnp.sum(norms, axis=1, keepdims=True)
        + jnp.sum(norms, axis=0, keepdims=True)
        - 2.0 * products
    )
    inner[...] = jnp.exp(-distance * inv_band)
    near_rows = rows_of(hi * 2 * rows, 2 * rows)
    far_rows = rows_of((1 - hi) * 2 * rows, 2 * rows)
    near_cols = cols_of(hi * 2 * rows, 2 * rows)

    def dot(left, right):
        return jnp.dot(left, right, precision=HIGHEST, preferred_element_type=jnp.float32)

    s_swap.wait()
    s_keep.wait()
    last = step_cols * MAIN_PARTS
    last_count = step_cols * LAST_PARTS
    last_cols = pl.ds(last, last_count)
    product[...] = dot(inner[far_rows, near_cols], s_all[near_rows, last_cols])
    far_copies = [
        send(product.at[pl.ds(slot * rows, rows)], far.at[lo], (far_send.at[slot], far_recv.at[lo]), across[slot])
        for slot in range(2)
    ]
    @pl.when(lo == 1)
    def _():
        far_copies[0].start()
        far_copies[1].start()

    @pl.when(lo == 0)
    def _():
        far_copies[1].start()
        far_copies[0].start()


    step_size = step_ref[0, 0]
    pull = 2.0 * inv_band * jnp.sum(inner[near_rows, :], axis=1, keepdims=True)
    loads[3].wait()
    x_swap.wait()

    def out_cols(u):
        return cols_of(half * lo + step_cols * u, step_cols)

    def out_swap(u):
        return send(
            result.at[rows_of((1 - lo) * rows, rows), cols_of(step_cols * u, step_cols)],
            moved.at[:, out_cols(u)],
            (out_send.at[u], out_recv.at[u]),
            sibling,
        )

    def finish(u, attracted):
        cols = cols_of(step_cols * u, step_cols)
        x = x_chip[:, cols]
        result[:, cols] = x + step_size * ((attracted + pull * x) * (1.0 / every))
        out_swap(u).start()
        moved[:, out_cols(u)] = result[rows_of(lo * rows, rows), cols]

    for u in range(MAIN_PARTS, STEP_PARTS):
        part_cols = pl.ds(step_cols * u, step_cols)
        finish(u, dot(inner[near_rows, near_cols], s_all[near_rows, part_cols]))

    @pl.loop(0, MAIN_PARTS)
    def _(u):
        for sem in range(2):
            step_recv(sem, u).wait()
        finish(u, dot(inner[near_rows, :], s_all[:, cols_of(step_cols * u, step_cols)]))

    @pl.loop(0, MAIN_PARTS)
    def _(u):
        for slot in range(2):
            step_copy(slot, u).wait_send()

    @pl.loop(0, GRAM_PARTS)
    def _(c):
        for slot in range(3):
            gram_copy(slot, c).wait_send()

    @pl.loop(0, STEP_PARTS)
    def _(u):
        out_swap(u).wait()

    for slot in range(2):
        pltpu.make_async_copy(far.at[slot], far.at[slot], far_recv.at[slot]).wait()
        cols = pl.ds(half * slot + last, last_count)
        moved[:, cols] = moved[:, cols] + step_size * (far[slot] * (1.0 / every))
    for copy in far_copies:
        copy.wait_send()


def on_device(dims, width, step_size, particles, gradients):
    rows, cells, nx, nz = dims
    every, half = 4 * rows, cells // 2
    n_x = every // nx
    n_z = n_x // nz
    f32 = jnp.float32
    sem = pltpu.SemaphoreType.DMA
    messages = 5 + 2 * (nx - 1) + 2 * (nz - 1)
    return pl.pallas_call(
        functools.partial(kernel, dims),
        out_shape=pltpu.VMEM((rows, cells), f32),
        in_specs=[pl.BlockSpec(memory_space=pltpu.HBM)] * 4,
        out_specs=pl.BlockSpec(memory_space=pltpu.VMEM),
        scratch_shapes=[
            pltpu.VMEM((rows, cells), f32),
            pltpu.VMEM((rows, cells), f32),
            pltpu.VMEM((every, cells // 4), f32),
            pltpu.VMEM((2 * rows, half), f32),
            pltpu.VMEM((every, half), f32),
            pltpu.VMEM((2 * rows, half), f32),
            pltpu.VMEM((2 * rows, half // STEP_PARTS * LAST_PARTS), f32),
            pltpu.VMEM((2, rows, half // STEP_PARTS * LAST_PARTS), f32),
            pltpu.VMEM((every, every), f32),
            pltpu.VMEM((every, every), f32),
            pltpu.VMEM((nx, n_x, every), f32),
            pltpu.VMEM((nz, n_z, every), f32),
            pltpu.VMEM((3, n_z // 2, every), f32),
            pltpu.VMEM((every, every), f32),
            pltpu.SMEM((1, 1), f32),
            pltpu.SMEM((1, 1), f32),
            pltpu.SemaphoreType.REGULAR,
            sem((7,)),
            sem((3, GRAM_PARTS)),
            sem((3, GRAM_PARTS)),
            sem((2,)),
            sem((2,)),
            sem((2, STEP_PARTS)),
            sem((2, STEP_PARTS)),
            sem((2, messages)),
            sem((STEP_PARTS,)),
            sem((STEP_PARTS,)),
            sem((2,)),
            sem((2,)),
        ],
        compiler_params=pltpu.CompilerParams(
            collective_id=0, has_side_effects=True, vmem_limit_bytes=52 * 2**20
        ),
        cost_estimate=pl.CostEstimate(
            flops=4 * every * every * cells // 4,
            bytes_accessed=5 * 4 * rows * cells,
            transcendentals=2 * rows * every,
        ),
    )(
        width.reshape(1, 1),
        step_size.reshape(1, 1),
        particles,
        gradients,
    )


def solution(mesh):
    def step(particles, gradients, width, step_size):
        rows, cells = particles.shape
        nz = NZ if mesh.shape["cell"] == NX * NYH * NZ else 1
        nx = mesh.shape["cell"] // NYH // nz
        return on_device((rows, cells, nx, nz), width, step_size, particles, gradients)

    in_specs = (P("dom", "cell"), P("dom", "cell"), P(), P())
    out_specs = P("dom", "cell")
    return jax.shard_map(step, mesh=mesh, in_specs=in_specs, out_specs=out_specs, check_vma=False)
```

```python
import functools

import jax
import jax.numpy as jnp
from jax import lax
from jax.experimental import pallas as pl
from jax.experimental.pallas import tpu as pltpu
from jax.sharding import PartitionSpec as P

MESH = pl.DeviceIdType.MESH
HIGHEST = lax.Precision.HIGHEST
NX, NYH, NZ = 4, 2, 4
GRAM_PARTS = 4
STEP_PARTS = 8
MAIN_PARTS = STEP_PARTS - 1
EARLY_PARTS = 3


def kernel(
    dims,
    width_hbm,
    step_hbm,
    particles,
    gradients,
    moved,
    x_own,
    s_own,
    x_gram,
    x_chip,
    s_all,
    result,
    product,
    far,
    part,
    sum_core,
    sum_x,
    sum_z,
    sum_y,
    inner,
    width_ref,
    step_ref,
    ready,
    load_sem,
    x_send,
    x_recv,
    xc_sem,
    ss_sem,
    s_send,
    s_recv,
    red_sem,
    out_send,
    out_recv,
    far_send,
    far_recv,
):
    rows, cells, nx, nz = dims
    every = 4 * rows
    half, quarter = cells // 2, cells // 4
    gram_cols, step_cols = quarter // GRAM_PARTS, half // STEP_PARTS
    dom, cell = lax.axis_index("dom"), lax.axis_index("cell")
    hi, lo = dom // 2, lax.rem(dom, 2)
    cx, cy, cz = cell // (NYH * nz), lax.rem(cell // nz, NYH), lax.rem(cell, nz)

    def cell_of(x, y, z):
        return (x * NYH + y) * nz + z

    sibling = (hi * 2 + 1 - lo, cell)
    across = [((1 - hi) * 2, cell), ((1 - hi) * 2 + 1, cell)]
    along_x = [lax.rem(cx + d, nx) for d in range(1, nx)]
    along_z = [lax.rem(cz + d, nz) for d in range(1, nz)]
    x_peers = [(dom, cell_of(x, cy, cz)) for x in along_x]
    z_peers = [(dom, cell_of(cx, cy, z)) for z in along_z]
    y_near = ((1 - hi) * 2 + lo, cell_of(cx, 1 - cy, cz))
    y_pair = ((1 - hi) * 2 + lo, cell)

    def send(src, dst, sems, to):
        return pltpu.make_async_remote_copy(
            src_ref=src,
            dst_ref=dst,
            send_sem=sems[0],
            recv_sem=sems[1],
            device_id=to,
            device_id_type=MESH,
        )

    def rows_of(index, count):
        return pl.ds(pl.multiple_of(index, count), count)

    def cols_of(index, count):
        return pl.ds(pl.multiple_of(index, count), count)

    def signal(sem, to):
        pl.semaphore_signal(sem, inc=1, device_id=to, device_id_type=MESH)

    cross_peers = [*x_peers, *z_peers, y_near]
    barrier = pltpu.get_barrier_semaphore()
    signal(barrier, y_pair)

    @pl.when(lo == 0)
    def _():
        for peer in cross_peers:
            signal(barrier, peer)

    my_rows = rows_of(dom * rows, rows)
    loads = [
        pltpu.make_async_copy(particles, x_own, load_sem.at[0]),
        pltpu.make_async_copy(gradients, s_own, load_sem.at[1]),
        pltpu.make_async_copy(
            particles.at[:, cols_of(half * lo + quarter * hi, quarter)],
            x_gram.at[my_rows],
            load_sem.at[2],
        ),
        pltpu.make_async_copy(
            particles.at[:, cols_of(half * lo, half)],
            x_chip.at[rows_of(lo * rows, rows)],
            load_sem.at[3],
        ),
        pltpu.make_async_copy(width_hbm, width_ref, load_sem.at[5]),
        pltpu.make_async_copy(step_hbm, step_ref, load_sem.at[6]),
    ]
    def gram_copy(slot, c):
        to = (across + [sibling])[slot]
        to_hi, to_lo = (hi, 1 - lo) if slot == 2 else (1 - hi, slot)
        start = half * to_lo + quarter * to_hi + gram_cols * c
        sem = lo if slot < 2 else 2
        return pltpu.make_async_remote_copy(
            src_ref=particles.at[:, cols_of(start, gram_cols)],
            dst_ref=x_gram.at[my_rows, cols_of(gram_cols * c, gram_cols)],
            send_sem=x_send.at[slot, c],
            recv_sem=x_recv.at[sem, c],
            device_id=to,
            device_id_type=MESH,
        )

    def gram_recv(sem, c):
        block = x_gram.at[pl.ds(0, rows), cols_of(gram_cols * c, gram_cols)]
        return pltpu.make_async_copy(block, block, x_recv.at[sem, c])

    @pl.when(lo == 1)
    def _():
        pl.semaphore_wait(barrier, 1)
        signal(barrier, sibling)
        for c in range(GRAM_PARTS):
            gram_copy(1, c).start()
        pl.semaphore_wait(ready, 1)

    @pl.when(lo == 0)
    def _():
        pl.semaphore_wait(barrier, 2 + len(cross_peers))
        signal(ready, sibling)
        for c in range(GRAM_PARTS):
            gram_copy(1, c).start()

    for c in range(GRAM_PARTS):
        gram_copy(0, c).start()
        gram_copy(2, c).start()
    for load in loads:
        load.start()
    x_swap = send(
        particles.at[:, cols_of(half * (1 - lo), half)],
        x_chip.at[rows_of(lo * rows, rows)],
        (xc_sem.at[0], xc_sem.at[1]),
        sibling,
    )
    x_swap.start()

    loads[4].wait()
    loads[5].wait()
    inv_band = 1.0 / width_ref[0, 0]
    loads[0].wait()
    loads[1].wait()

    @pl.loop(0, STEP_PARTS * 2)
    def _(u):
        cols = cols_of(u * step_cols, step_cols)
        s_own[:, cols] = s_own[:, cols] - 2.0 * inv_band * x_own[:, cols]

    def step_copy(slot, u):
        return pltpu.make_async_remote_copy(
            src_ref=s_own.at[:, cols_of(half * slot + step_cols * u, step_cols)],
            dst_ref=s_all.at[my_rows, cols_of(step_cols * u, step_cols)],
            send_sem=s_send.at[slot, u],
            recv_sem=s_recv.at[lo, u],
            device_id=across[slot],
            device_id_type=MESH,
        )

    def step_recv(sem, u):
        block = s_all.at[pl.ds(0, rows), cols_of(step_cols * u, step_cols)]
        return pltpu.make_async_copy(block, block, s_recv.at[sem, u])

    @pl.loop(0, EARLY_PARTS)
    def _(u):
        for slot in range(2):
            step_copy(slot, u).start()

    s_swap = send(
        s_own.at[:, cols_of(half * (1 - lo), half)],
        s_all.at[my_rows],
        (ss_sem.at[0], ss_sem.at[1]),
        sibling,
    )
    s_swap.start()
    s_keep = pltpu.make_async_copy(
        s_own.at[:, cols_of(half * lo, half)], s_all.at[my_rows], load_sem.at[4]
    )
    s_keep.start()

    loads[2].wait()
    part[...] = jnp.zeros_like(part)

    @pl.loop(0, GRAM_PARTS)
    def _(c):
        for sem in range(3):
            if sem == 2:
                gram_recv(2, c).wait()
            else:
                gram_recv(sem, c).wait()
        block = x_gram[:, cols_of(gram_cols * c, gram_cols)]
        part[...] += lax.dot_general(
            block,
            block,
            (((1,), (1,)), ((), ())),
            precision=HIGHEST,
            preferred_element_type=jnp.float32,
        )

    n_x, n_z, n_y = every // nx, every // nx // nz, every // nx // nz // 2
    count = [0]

    def sems():
        k = count[0]
        count[0] += 1
        return red_sem.at[0, k], red_sem.at[1, k]

    def later_parts():
        @pl.loop(EARLY_PARTS, MAIN_PARTS)
        def _(u):
            for slot in range(2):
                step_copy(slot, u).start()

    to_core = send(part, sum_core, sems(), sibling)
    from_core = send(inner, inner, sems(), sibling)

    @pl.when(lo == 1)
    def _():
        to_core.start()
        to_core.wait_send()
        later_parts()
        from_core.wait_recv()

    @pl.when(lo == 0)
    def _():
        to_core.wait_recv()
        sum_core[...] += part[...]
        copies = [
            send(sum_core.at[rows_of(x * n_x, n_x)], sum_x.at[d], sems(), peer)
            for d, (x, peer) in enumerate(zip(along_x, x_peers, strict=True))
        ]
        for copy in copies:
            copy.start()
        total = sum_core[rows_of(cx * n_x, n_x), :]
        for d, copy in enumerate(copies):
            copy.wait()
            total = total + sum_x[d]
        sum_x[nx - 1] = total

        copies = [
            send(sum_x.at[nx - 1, rows_of(z * n_z, n_z)], sum_z.at[d], sems(), peer)
            for d, (z, peer) in enumerate(zip(along_z, z_peers, strict=True))
        ]
        for copy in copies:
            copy.start()
        total = sum_x[nx - 1, rows_of(cz * n_z, n_z), :]
        for d, copy in enumerate(copies):
            copy.wait()
            total = total + sum_z[d]
        sum_z[nz - 1] = total

        swap = send(sum_z.at[nz - 1, rows_of((1 - cy) * n_y, n_y)], sum_y.at[0], sems(), y_near)
        swap.start()
        swap.wait()
        sum_y[1] = sum_y[0] + sum_z[nz - 1, rows_of(cy * n_y, n_y), :]
        swap = send(sum_y.at[1], sum_y.at[2], sems(), y_pair)
        swap.start()
        later_parts()
        swap.wait()
        y_rows = rows_of(cx * n_x + cz * n_z + cy * n_y, n_y)
        z_rows = rows_of(cx * n_x + cz * n_z, n_z)
        x_rows = rows_of(cx * n_x, n_x)
        inner[y_rows, :] = sum_y[1] + sum_y[2]
        for block, peers in ((y_rows, [y_near]), (z_rows, z_peers), (x_rows, x_peers)):
            copies = [send(inner.at[block], inner.at[block], sems(), peer) for peer in peers]
            for copy in copies:
                copy.start()
            for copy in copies:
                copy.wait()
        from_core.start()
        from_core.wait_send()

    products = inner[...]
    i = lax.broadcasted_iota(jnp.int32, (every, every), 0)
    j = lax.broadcasted_iota(jnp.int32, (every, every), 1)
    norms = jnp.where(i == j, products, 0.0)
    distance = (
        jnp.sum(norms, axis=1, keepdims=True)
        + jnp.sum(norms, axis=0, keepdims=True)
        - 2.0 * products
    )
    inner[...] = jnp.exp(-distance * inv_band)
    near_rows = rows_of(hi * 2 * rows, 2 * rows)
    far_rows = rows_of((1 - hi) * 2 * rows, 2 * rows)
    near_cols = cols_of(hi * 2 * rows, 2 * rows)

    def dot(left, right):
        return jnp.dot(left, right, precision=HIGHEST, preferred_element_type=jnp.float32)

    s_swap.wait()
    s_keep.wait()
    last = step_cols * MAIN_PARTS
    last_cols = pl.ds(last, step_cols)
    product[...] = dot(inner[far_rows, near_cols], s_all[near_rows, last_cols])
    piece = step_cols // 2

    def far_copy(slot, k):
        cols = pl.ds(piece * k, piece)
        return send(
            product.at[pl.ds(slot * rows, rows), cols],
            far.at[lo, :, cols],
            (far_send.at[slot, k], far_recv.at[lo, k]),
            across[slot],
        )

    @pl.when(lo == 0)
    def _():
        for k in range(2):
            far_copy(1, k).start()
            far_copy(0, k).start()

    @pl.when(lo == 1)
    def _():
        for k in range(2):
            far_copy(0, k).start()
            far_copy(1, k).start()

    step_size = step_ref[0, 0]
    pull = 2.0 * inv_band * jnp.sum(inner[near_rows, :], axis=1, keepdims=True)
    loads[3].wait()
    x_swap.wait()

    def out_cols(u):
        return cols_of(half * lo + step_cols * u, step_cols)

    def out_swap(u):
        return send(
            result.at[rows_of((1 - lo) * rows, rows), cols_of(step_cols * u, step_cols)],
            moved.at[:, out_cols(u)],
            (out_send.at[u], out_recv.at[u]),
            sibling,
        )

    def finish(u, attracted):
        cols = cols_of(step_cols * u, step_cols)
        x = x_chip[:, cols]
        result[:, cols] = x + step_size * ((attracted + pull * x) * (1.0 / every))
        out_swap(u).start()
        moved[:, out_cols(u)] = result[rows_of(lo * rows, rows), cols]

    finish(MAIN_PARTS, dot(inner[near_rows, near_cols], s_all[near_rows, last_cols]))

    @pl.loop(0, MAIN_PARTS)
    def _(u):
        for sem in range(2):
            step_recv(sem, u).wait()
        finish(u, dot(inner[near_rows, :], s_all[:, cols_of(step_cols * u, step_cols)]))

    @pl.loop(0, MAIN_PARTS)
    def _(u):
        for slot in range(2):
            step_copy(slot, u).wait_send()

    @pl.loop(0, GRAM_PARTS)
    def _(c):
        for slot in range(3):
            gram_copy(slot, c).wait_send()

    @pl.loop(0, STEP_PARTS)
    def _(u):
        out_swap(u).wait()

    for slot in range(2):
        for k in range(2):
            block = far.at[slot, :, pl.ds(piece * k, piece)]
            pltpu.make_async_copy(block, block, far_recv.at[slot, k]).wait()
        cols = pl.ds(half * slot + last, step_cols)
        moved[:, cols] = moved[:, cols] + step_size * (far[slot] * (1.0 / every))
    for slot in range(2):
        for k in range(2):
            far_copy(slot, k).wait_send()


def on_device(dims, width, step_size, particles, gradients):
    rows, cells, nx, nz = dims
    every, half = 4 * rows, cells // 2
    n_x = every // nx
    n_z = n_x // nz
    f32 = jnp.float32
    sem = pltpu.SemaphoreType.DMA
    messages = 5 + 2 * (nx - 1) + 2 * (nz - 1)
    return pl.pallas_call(
        functools.partial(kernel, dims),
        out_shape=pltpu.VMEM((rows, cells), f32),
        in_specs=[pl.BlockSpec(memory_space=pltpu.HBM)] * 4,
        out_specs=pl.BlockSpec(memory_space=pltpu.VMEM),
        scratch_shapes=[
            pltpu.VMEM((rows, cells), f32),
            pltpu.VMEM((rows, cells), f32),
            pltpu.VMEM((every, cells // 4), f32),
            pltpu.VMEM((2 * rows, half), f32),
            pltpu.VMEM((every, half), f32),
            pltpu.VMEM((2 * rows, half), f32),
            pltpu.VMEM((2 * rows, half // STEP_PARTS), f32),
            pltpu.VMEM((2, rows, half // STEP_PARTS), f32),
            pltpu.VMEM((every, every), f32),
            pltpu.VMEM((every, every), f32),
            pltpu.VMEM((nx, n_x, every), f32),
            pltpu.VMEM((nz, n_z, every), f32),
            pltpu.VMEM((3, n_z // 2, every), f32),
            pltpu.VMEM((every, every), f32),
            pltpu.SMEM((1, 1), f32),
            pltpu.SMEM((1, 1), f32),
            pltpu.SemaphoreType.REGULAR,
            sem((7,)),
            sem((3, GRAM_PARTS)),
            sem((3, GRAM_PARTS)),
            sem((2,)),
            sem((2,)),
            sem((2, STEP_PARTS)),
            sem((2, STEP_PARTS)),
            sem((2, messages)),
            sem((STEP_PARTS,)),
            sem((STEP_PARTS,)),
            sem((2, 2)),
            sem((2, 2)),
        ],
        compiler_params=pltpu.CompilerParams(
            collective_id=0, has_side_effects=True, vmem_limit_bytes=52 * 2**20
        ),
        cost_estimate=pl.CostEstimate(
            flops=4 * every * every * cells // 4,
            bytes_accessed=5 * 4 * rows * cells,
            transcendentals=2 * rows * every,
        ),
    )(
        width.reshape(1, 1),
        step_size.reshape(1, 1),
        particles,
        gradients,
    )


def solution(mesh):
    def step(particles, gradients, width, step_size):
        rows, cells = particles.shape
        nz = NZ if mesh.shape["cell"] == NX * NYH * NZ else 1
        nx = mesh.shape["cell"] // NYH // nz
        return on_device((rows, cells, nx, nz), width, step_size, particles, gradients)

    in_specs = (P("dom", "cell"), P("dom", "cell"), P(), P())
    out_specs = P("dom", "cell")
    return jax.shard_map(step, mesh=mesh, in_specs=in_specs, out_specs=out_specs, check_vma=False)
```
